256 devices in a mesh: pairs: 256 (over x, y, z, core).
Axes of the slice: x: 4, y: 4, z: 8, core: 2. Of those that a mesh axis runs over, the one named last changes fastest.
Arguments:
- image_feats: bfloat16 [65536, 768], P('pairs'), may hold values from -6 to 6
- text_feats: bfloat16 [65536, 768], P('pairs'), may hold values from -6 to 6
- image_head: bfloat16 [768, 768], replicated, may hold values from -0.0078125 to 0.0078125
- text_head: bfloat16 [768, 768], replicated, may hold values from -0.0078125 to 0.0078125
- logit_scale: float32 [1], replicated, may hold values from 4 to 16
- logit_bias: float32 [1], replicated, may hold values from -6 to -2
- round_offsets: int32 [4], replicated, may hold values from 1 to 255, as said below
Outputs:
- image_grad: bfloat16 [65536, 768], P('pairs')
- text_grad: bfloat16 [65536, 768], P('pairs')
- image_head_grad: float32 [768, 768], replicated
- text_head_grad: float32 [768, 768], replicated
- scalar_grads: float32 [3], replicated
The draws below stay inside these ranges and needn't reach their ends.
Inputs may be any that keep to these rules, and one draw needn't show every extreme that they name: `round_offsets`: the 4 offsets are distinct; 1 and 256 - 1 are among them.
All inputs are finite; a program needn't handle non-finite values.
Results may differ from the reference program's by a relative error of at most 0.0065.
Values may be sent and summed in bfloat16 or wider, within the bound.
No kernel may reach another device: no remote copies, remote signals or barrier semaphores. Data moves between devices by JAX's collectives and lax.ppermute only.
A program may use at most 128 MiB of HBM per device.

```python
import math
import jax
import jax.numpy as jnp
from jax import lax

D = 768
TOK_DEV = 256
ROUNDS = 4
TOKENS = 65536
N_PAIRS = 256


def draw_round_offsets(key, part):
    key = jax.random.fold_in(key, 11)
    first_key, second_key = jax.random.split(key)
    middle = jax.random.permutation(first_key, N_PAIRS - 3)[:ROUNDS - 2] + 2
    values = jnp.concatenate([jnp.array([1, N_PAIRS - 1], jnp.int32), middle.astype(jnp.int32)])
    order = jax.random.permutation(second_key, ROUNDS)
    return values[order].astype(jnp.int32)


def levels(rng, dims, cuts, low, largest):
    def one(axis_at, shards_of):
        draws = jax.random.uniform(jax.random.fold_in(jax.random.fold_in(rng, 6), axis_at), (shards_of,), jnp.float32, low / len(cuts), largest / len(cuts))
        return jnp.repeat(jnp.exp(draws), dims[axis_at] // shards_of).reshape((-1,) + (1,) * (len(dims) - axis_at - 1))

    level = one(*cuts[0])
    for cut in cuts[1:]:
        level = level * one(*cut)
    return level


def normal_values(stream_key, extent, width, most, cuts=(), kind=jnp.bfloat16):
    values = jax.random.normal(stream_key, extent, jnp.float32) * width
    if len(cuts) > 0:
        values = levels(stream_key, extent, cuts, -0.22, 0.18) * values
    return jnp.clip(values, min=-most, max=most).astype(kind)


def setup_inputs(seed: int = 0) -> dict:
    arg_keys = jax.random.split(jax.random.key(seed), 8)
    image_feats = normal_values(arg_keys[0], (TOKENS, D), 1.0, 6.0, ((0, 256),))
    text_feats = normal_values(arg_keys[1], (TOKENS, D), 1.0, 6.0, ((0, 256),))
    image_head = normal_values(arg_keys[2], (D, D), (D * D) ** -0.5, 0.0078125)
    text_head = normal_values(arg_keys[3], (D, D), (D * D) ** -0.5, 0.0078125)
    logit_scale = jnp.clip(jnp.exp(jax.random.uniform(arg_keys[4], (1,), jnp.float32, math.log(4.0), math.log(16.0))), 4.0, 16.0)
    logit_bias = jnp.clip(jax.random.uniform(arg_keys[5], (1,), jnp.float32, -6.0, -2.0), -6.0, -2.0)
    round_offsets = draw_round_offsets(jax.random.fold_in(arg_keys[7], 71), 0)
    return {"image_feats": image_feats, "text_feats": text_feats, "image_head": image_head, "text_head": text_head, "logit_scale": logit_scale, "logit_bias": logit_bias, "round_offsets": round_offsets}


EPS = 1e-06

def embed(feats, head):
    proj = jnp.dot(feats, head, preferred_element_type=jnp.float32)
    norms = jnp.sqrt(lax.optimization_barrier(jnp.sum(proj * proj, axis=-1, keepdims=True)) + EPS)
    return (proj / norms, norms)

def score_tile(left, right, scale, bias, own):
    cosine = jnp.dot(left, right.T, preferred_element_type=jnp.float32)
    logit = scale * cosine + bias
    rows = left.shape[0]
    eye = (jnp.arange(rows)[:, None] == jnp.arange(rows)[None, :]).astype(jnp.float32)
    label = 2.0 * eye - 1.0 if own else -jnp.ones_like(logit)
    loss = jnp.sum(jax.nn.softplus(-label * logit))
    dlogit = -label * jax.nn.sigmoid(-label * logit)
    coef = (scale * dlogit).astype(jnp.bfloat16)
    return (loss, jnp.sum(dlogit * cosine), jnp.sum(dlogit), coef)

def backnorm(zhat, norms, grad):
    inner = lax.optimization_barrier(jnp.sum(zhat * grad, axis=-1, keepdims=True))
    return ((grad - zhat * inner) / norms).astype(jnp.bfloat16)

def reference(image_feats, text_feats, image_head, text_head, logit_scale, logit_bias, round_offsets):
    scale = logit_scale[0]
    bias = logit_bias[0]
    rows = TOK_DEV
    zhat_img_all, _ = embed(image_feats, image_head)
    zhat_txt_all, _ = embed(text_feats, text_head)
    z_img_all = zhat_img_all.astype(jnp.bfloat16)
    z_txt_all = zhat_txt_all.astype(jnp.bfloat16)

    def group_rows(table, group):
        return lax.dynamic_slice_in_dim(table, (group * rows).astype(jnp.int32), rows, 0)

    def step(carry, group):
        sum_wi, sum_wt, stats = carry
        x_img = group_rows(image_feats, group)
        x_txt = group_rows(text_feats, group)
        zh_img, n_img = embed(x_img, image_head)
        zh_txt, n_txt = embed(x_txt, text_head)
        z_img = group_rows(z_img_all, group)
        z_txt = group_rows(z_txt_all, group)
        loss, gscale, gbias, coef = score_tile(z_img, z_txt, scale, bias, True)
        dz_img = jnp.dot(coef, z_txt, preferred_element_type=jnp.float32)
        dz_txt = jnp.dot(coef.T, z_img, preferred_element_type=jnp.float32)
        for turn in range(ROUNDS):
            offset_now = round_offsets[turn].astype(jnp.int32)
            ahead = jnp.mod(group + offset_now, N_PAIRS).astype(jnp.int32)
            behind = jnp.mod(group - offset_now + N_PAIRS, N_PAIRS).astype(jnp.int32)
            p_txt = group_rows(z_txt_all, ahead)
            p_img = group_rows(z_img_all, behind)
            part_loss, part_scale, part_bias, coef = score_tile(z_img, p_txt, scale, bias, False)
            loss = loss + part_loss
            gscale = gscale + part_scale
            gbias = gbias + part_bias
            dz_img = dz_img + jnp.dot(coef, p_txt, preferred_element_type=jnp.float32)
            _, _, _, coef_back = score_tile(p_img, z_txt, scale, bias, False)
            back = jnp.dot(coef_back.T, p_img, preferred_element_type=jnp.float32).astype(jnp.bfloat16)
            dz_txt = dz_txt + lax.optimization_barrier(back).astype(jnp.float32)
        du_img = backnorm(zh_img, n_img, dz_img)
        du_txt = backnorm(zh_txt, n_txt, dz_txt)
        g_img = jnp.dot(du_img, image_head.T, preferred_element_type=jnp.float32).astype(jnp.bfloat16)
        g_txt = jnp.dot(du_txt, text_head.T, preferred_element_type=jnp.float32).astype(jnp.bfloat16)
        sum_wi = sum_wi + jnp.dot(x_img.T, du_img, preferred_element_type=jnp.float32)
        sum_wt = sum_wt + jnp.dot(x_txt.T, du_txt, preferred_element_type=jnp.float32)
        stats = stats + jnp.stack([loss, gscale, gbias])
        return ((sum_wi, sum_wt, stats), (g_img, g_txt))
    start = (jnp.zeros((D, D), jnp.float32), jnp.zeros((D, D), jnp.float32), jnp.zeros((3,), jnp.float32))
    groups = jnp.arange(N_PAIRS).astype(jnp.int32)
    (sum_wi, sum_wt, stats), (g_img, g_txt) = lax.scan(step, start, groups)
    total = float(TOKENS)
    return (g_img.reshape(TOKENS, D), g_txt.reshape(TOKENS, D), sum_wi / total, sum_wt / total, stats / total)
```

```python
import jax
import jax.numpy as jnp
from jax import lax
from jax.experimental import pallas as pl
from jax.experimental.pallas import tpu as pltpu
from jax.sharding import PartitionSpec as P

EPS = 1e-06
X, Y, Z, CORES = 4, 4, 8, 2
COUNT = X * Y * Z * CORES
STEP = Z * CORES
HALF = STEP // 2

PLANES = [[xy * STEP + zc for xy in range(X * Y)] for zc in range(STEP)]
COLUMNS = [[xy * STEP + z * CORES + c for z in range(Z)] for xy in range(X * Y) for c in range(CORES)]


def shifted(value, steps):
    return lax.ppermute(value, "pairs", [(source, (source + steps) % COUNT) for source in range(COUNT)])


def other_core(value):
    return lax.ppermute(value, "pairs", [(source, source ^ 1) for source in range(COUNT)])


def exchange(value, groups):
    return lax.all_to_all(value, "pairs", 0, 0, axis_index_groups=groups, tiled=True)


def embed_kernel(xi_ref, xt_ref, wi_ref, wt_ref, zi_ref, zt_ref, both_ref, zh_ref, n_ref):
    for k, (x_ref, w_ref, z_ref) in enumerate(((xi_ref, wi_ref, zi_ref), (xt_ref, wt_ref, zt_ref))):
        rows = x_ref.shape[0]
        at = slice(k * rows, (k + 1) * rows)
        proj = jnp.dot(x_ref[...], w_ref[...], preferred_element_type=jnp.float32)
        norms = jnp.sqrt(jnp.sum(proj * proj, axis=-1, keepdims=True) + EPS)
        zh = proj / norms
        z = zh.astype(jnp.bfloat16)
        n_ref[at, :] = norms
        zh_ref[at, :] = zh
        z_ref[...] = z
        both_ref[at, :] = z


def embed(image_feats, text_feats, image_head, text_head):
    rows, width = image_feats.shape
    vmem = pl.BlockSpec(memory_space=pltpu.VMEM)
    return pl.pallas_call(
        embed_kernel,
        out_shape=(
            jax.ShapeDtypeStruct((rows, width), jnp.bfloat16),
            jax.ShapeDtypeStruct((rows, width), jnp.bfloat16),
            jax.ShapeDtypeStruct((2 * rows, width), jnp.bfloat16),
            jax.ShapeDtypeStruct((2 * rows, width), jnp.float32),
            jax.ShapeDtypeStruct((2 * rows, 1), jnp.float32),
        ),
        in_specs=[vmem] * 4,
        out_specs=(vmem,) * 5,
        compiler_params=pltpu.CompilerParams(vmem_limit_bytes=32 * 1024 * 1024),
        name="embed",
    )(image_feats, text_feats, image_head, text_head)


def swap(z_img, z_txt, offset):
    low = jnp.mod(offset + HALF, STEP)
    high = jnp.mod((offset + HALF) // STEP, COUNT // STEP)

    def branch(steps):
        if steps == 0:
            return lambda txt, img: (txt, img)
        return lambda txt, img: (shifted(txt, -steps), shifted(img, steps))

    txt, img = lax.switch(low, [branch(k - HALF) for k in range(STEP)], z_txt, z_img)
    return tuple(lax.switch(high, [branch(k * STEP) for k in range(COUNT // STEP)], txt, img))


def dot_t(left, right):
    return lax.dot_general(left, right, (((1,), (1,)), ((), ())), preferred_element_type=jnp.float32)


def tiles_kernel(sb_ref, core_ref, zi_ref, zt_ref, zh_ref, n_ref, ahead_ref, behind_ref, t3_ref, i3_ref, t4_ref, i4_ref,
                 xi_ref, xt_ref, dui_ref, dut_ref, kept_ref, given_ref):
    scale = sb_ref[0]
    bias = sb_ref[1]
    zi = zi_ref[...]
    zt = zt_ref[...]
    rows = zi.shape[0]
    own = lax.broadcasted_iota(jnp.int32, (rows, rows), 0) == lax.broadcasted_iota(jnp.int32, (rows, rows), 1)

    def gate(cosine, mine):
        logit = scale * cosine + bias
        v = jnp.where(own, -logit, logit) if mine else logit
        e = jnp.exp(-jnp.abs(v))
        inv = 1.0 / (1.0 + e)
        dlogit = jnp.where(v >= 0, inv, e * inv)
        if mine:
            dlogit = jnp.where(own, -dlogit, dlogit)
        return v, e, dlogit

    def fold(x):
        return jnp.sum(x.reshape(rows // 8, 8, rows), axis=0)

    loss = gscale = gbias = None
    dz_img = dz_txt = None
    images, texts = slice(0, rows), slice(rows, 2 * rows)
    pairs = (
        (lambda: zt, lambda: zi),
        (lambda: ahead_ref[texts, :], lambda: behind_ref[images, :]),
        (lambda: behind_ref[texts, :], lambda: ahead_ref[images, :]),
        (lambda: t3_ref[...], lambda: i3_ref[...]),
        (lambda: t4_ref[...], lambda: i4_ref[...]),
    )
    for k, (get_txt, get_img) in enumerate(pairs):
        txt = get_txt()
        cosine = dot_t(zi, txt)
        v, e, dlogit = gate(cosine, k == 0)
        parts = fold(jnp.maximum(v, 0.0) + jnp.log1p(e)), fold(dlogit * cosine), fold(dlogit)
        coef = (scale * dlogit).astype(jnp.bfloat16)
        to_img = jnp.dot(coef, txt, preferred_element_type=jnp.float32)
        img = get_img()
        if k == 0:
            coef_back = coef.T
        else:
            coef_back = (scale * gate(dot_t(zt, img), False)[2]).astype(jnp.bfloat16)
        to_txt = jnp.dot(coef_back, img, preferred_element_type=jnp.float32)
        if k == 0:
            loss, gscale, gbias = parts
            dz_img, dz_txt = to_img, to_txt
        else:
            loss, gscale, gbias = loss + parts[0], gscale + parts[1], gbias + parts[2]
            dz_img, dz_txt = dz_img + to_img, dz_txt + to_txt

    for dz, at, du_ref in ((dz_img, images, dui_ref), (dz_txt, texts, dut_ref)):
        zh = zh_ref[at, :]
        inner = jnp.sum(zh * dz, axis=-1, keepdims=True)
        du_ref[...] = ((dz - zh * inner) / n_ref[at, :]).astype(jnp.bfloat16)

    def head_grad(out_ref, x_ref, du_ref):
        width = x_ref.shape[1]
        out_ref[0:width, :] = lax.dot_general(
            x_ref[...], du_ref[...], (((0,), (0,)), ((), ())), preferred_element_type=jnp.float32
        )

    core = core_ref[0]

    @pl.when(core == 0)
    def _():
        head_grad(given_ref, xt_ref, dut_ref)
        head_grad(kept_ref, xi_ref, dui_ref)

    @pl.when(core == 1)
    def _():
        head_grad(given_ref, xi_ref, dui_ref)
        head_grad(kept_ref, xt_ref, dut_ref)

    at = lax.broadcasted_iota(jnp.int32, (8, kept_ref.shape[1]), 1)
    stats = jnp.where(at == 0, jnp.sum(loss), jnp.where(at == 1, jnp.sum(gscale), jnp.sum(gbias)))
    stats = jnp.where(at < 3, stats, 0.0)
    last = slice(kept_ref.shape[0] - 8, kept_ref.shape[0])
    kept_ref[last, :] = stats
    given_ref[last, :] = stats


def tiles(sb, core, z_img, z_txt, *others):
    rows, width = z_img.shape
    vmem = pl.BlockSpec(memory_space=pltpu.VMEM)
    return pl.pallas_call(
        tiles_kernel,
        out_shape=(
            jax.ShapeDtypeStruct((rows, width), jnp.bfloat16),
            jax.ShapeDtypeStruct((rows, width), jnp.bfloat16),
            jax.ShapeDtypeStruct((width + 8, width), jnp.float32),
            jax.ShapeDtypeStruct((width + 8, width), jnp.float32),
        ),
        in_specs=[pl.BlockSpec(memory_space=pltpu.SMEM)] * 2 + [vmem] * (2 + len(others)),
        out_specs=(vmem, vmem, vmem, vmem),
        compiler_params=pltpu.CompilerParams(vmem_limit_bytes=40 * 1024 * 1024),
        name="tiles",
    )(sb, core, z_img, z_txt, *others)


def summed_heads(given, kept, total):
    width = kept.shape[1]
    rows = width // (X * Y)
    both = kept + other_core(given)
    part = both[:width].astype(jnp.bfloat16)
    stats = both[width, 0:3]
    one = lax.reduce_precision(stats, 8, 7)
    two = lax.reduce_precision(stats - one, 8, 7)
    three = stats - one - two
    terms = jnp.stack([one, two, three])
    extra = jnp.zeros((8, width), jnp.bfloat16).at[0:3, 0:3].set(terms.astype(jnp.bfloat16))
    plane = jnp.concatenate([part.reshape(X * Y, rows, width), jnp.broadcast_to(extra[None], (X * Y, 8, width))], axis=1)
    plane = exchange(plane, PLANES)
    plane = jnp.sum(plane.astype(jnp.float32), axis=0)
    stats = jnp.sum(plane[rows : rows + 3, 0:3], axis=0)
    few = rows // Z
    extra = jnp.zeros((8 - few, width), jnp.float32).at[0, 0:3].set(stats)
    column = jnp.concatenate([plane[:rows].reshape(Z, few, width), jnp.broadcast_to(extra[None], (Z, 8 - few, width))], axis=1)
    column = jnp.sum(exchange(column, COLUMNS), axis=0) / total
    stats = column[few, 0:3]
    part = column[:few].astype(jnp.bfloat16)
    part = exchange(jnp.broadcast_to(part[None], (Z, few, width)), COLUMNS).reshape(rows, width)
    part = exchange(jnp.broadcast_to(part[None], (X * Y, rows, width)), PLANES).reshape(width, width)
    return part, stats


def local(image_feats, text_feats, image_head, text_head, logit_scale, logit_bias, round_offsets):
    total = float(COUNT * image_feats.shape[0])
    z_img, z_txt, both, zh, norms = embed(image_feats, text_feats, image_head, text_head)
    order = jnp.sort(round_offsets)
    ahead = shifted(both, -1)
    behind = shifted(both, 1)
    far = swap(z_img, z_txt, order[1]) + swap(z_img, z_txt, order[2])
    sb = jnp.concatenate([logit_scale, logit_bias])
    core = lax.axis_index("pairs") % CORES
    du_img, du_txt, kept, given = tiles(
        sb, core.reshape(1), z_img, z_txt, zh, norms, ahead, behind, *far, image_feats, text_feats
    )
    part, sum_stats = summed_heads(given, kept, total)
    first = core == 0
    theirs = other_core(part)
    sum_wi = jnp.where(first, part, theirs).astype(jnp.float32)
    sum_wt = jnp.where(first, theirs, part).astype(jnp.float32)

    g_img = jnp.dot(du_img, image_head.T, preferred_element_type=jnp.float32).astype(jnp.bfloat16)
    g_txt = jnp.dot(du_txt, text_head.T, preferred_element_type=jnp.float32).astype(jnp.bfloat16)
    return (g_img, g_txt, sum_wi, sum_wt, sum_stats)


def solution(mesh):
    placed = (P("pairs", None), P("pairs", None), P(), P(), P(), P(), P())
    return jax.shard_map(
        local,
        mesh=mesh,
        in_specs=placed,
        out_specs=(P("pairs", None), P("pairs", None), P(), P(), P()),
        check_vma=False,
    )
```

```python
import jax
import jax.numpy as jnp
from jax import lax
from jax.experimental import pallas as pl
from jax.experimental.pallas import tpu as pltpu
from jax.sharding import PartitionSpec as P

EPS = 1e-06
X, Y, Z, CORES = 4, 4, 8, 2
COUNT = X * Y * Z * CORES
STEP = Z * CORES
SPREAD = X * Y

PLANES = [[xy * STEP + zc for xy in range(X * Y)] for zc in range(STEP)]
COLUMNS = [[xy * STEP + z * CORES + c for z in range(Z)] for xy in range(X * Y) for c in range(CORES)]


def shifted(value, steps):
    return lax.ppermute(value, "pairs", [(source, (source + steps) % COUNT) for source in range(COUNT)])


def other_core(value):
    return lax.ppermute(value, "pairs", [(source, source ^ 1) for source in range(COUNT)])


def exchange(value, groups):
    return lax.all_to_all(value, "pairs", 0, 0, axis_index_groups=groups, tiled=True)


def embed_kernel(xi_ref, xt_ref, wi_ref, wt_ref, zi_ref, zt_ref, both_ref, zh_ref, n_ref):
    piece = both_ref.shape[1] // 2
    for k, (x_ref, w_ref, z_ref) in enumerate(((xi_ref, wi_ref, zi_ref), (xt_ref, wt_ref, zt_ref))):
        rows = x_ref.shape[0]
        at = slice(k * rows, (k + 1) * rows)
        proj = jnp.dot(x_ref[...], w_ref[...], preferred_element_type=jnp.float32)
        norms = jnp.sqrt(jnp.sum(proj * proj, axis=-1, keepdims=True) + EPS)
        zh = proj / norms
        z = zh.astype(jnp.bfloat16)
        n_ref[at, :] = norms
        zh_ref[at, :] = zh
        z_ref[...] = z
        both_ref[:, k * piece : (k + 1) * piece, :] = z.reshape(SPREAD, piece, z.shape[1])


def embed(image_feats, text_feats, image_head, text_head):
    rows, width = image_feats.shape
    vmem = pl.BlockSpec(memory_space=pltpu.VMEM)
    return pl.pallas_call(
        embed_kernel,
        out_shape=(
            jax.ShapeDtypeStruct((rows, width), jnp.bfloat16),
            jax.ShapeDtypeStruct((rows, width), jnp.bfloat16),
            jax.ShapeDtypeStruct((SPREAD, 2 * rows // SPREAD, width), jnp.bfloat16),
            jax.ShapeDtypeStruct((2 * rows, width), jnp.float32),
            jax.ShapeDtypeStruct((2 * rows, 1), jnp.float32),
        ),
        in_specs=[vmem] * 4,
        out_specs=(vmem,) * 5,
        compiler_params=pltpu.CompilerParams(vmem_limit_bytes=32 * 1024 * 1024),
        name="embed",
    )(image_feats, text_feats, image_head, text_head)


def turned(value, steps):
    pairs = [(source, source // STEP * STEP + (source + steps) % STEP) for source in range(COUNT)]
    return lax.ppermute(value, "pairs", pairs)


def along(txt, img, low):
    def branch(steps):
        if steps == 0:
            return lambda txt, img: (txt, img)
        return lambda txt, img: (turned(txt, -steps), turned(img, steps))

    return tuple(lax.switch(low, [branch(k) for k in range(STEP)], txt, img))


def line_up_kernel(at_ref, a_ref, b_ref, c_ref, d_ref, out_ref):
    piece = a_ref.shape[1]
    for k, ref in enumerate((a_ref, b_ref, c_ref, d_ref)):
        for p in range(SPREAD):
            out_ref[p, k * piece : (k + 1) * piece, :] = ref[lax.rem(at_ref[k] + p, SPREAD)]


def line_up(at, parts):
    vmem = pl.BlockSpec(memory_space=pltpu.VMEM)
    slots, piece, width = parts[0].shape
    return pl.pallas_call(
        line_up_kernel,
        out_shape=jax.ShapeDtypeStruct((slots, len(parts) * piece, width), parts[0].dtype),
        in_specs=[pl.BlockSpec(memory_space=pltpu.SMEM)] + [vmem] * len(parts),
        out_specs=vmem,
        compiler_params=pltpu.CompilerParams(vmem_limit_bytes=16 * 1024 * 1024),
        name="line_up",
    )(at, *parts)


def fetch(both, offsets):
    piece = both.shape[1] // 2
    place = lax.axis_index("pairs") % STEP
    spread = exchange(both, PLANES)
    img, txt = spread[:, :piece], spread[:, piece:]
    parts, at = [], []
    for offset in offsets:
        low, high = offset % STEP, offset // STEP
        parts += along(txt, img, low)
        at += [jnp.mod(high + (place + low) // STEP, SPREAD), jnp.mod(SPREAD - high - (place < low), SPREAD)]
    return exchange(line_up(jnp.stack(at).astype(jnp.int32), parts), PLANES)


def dot_t(left, right):
    return lax.dot_general(left, right, (((1,), (1,)), ((), ())), preferred_element_type=jnp.float32)


def tiles_kernel(sb_ref, core_ref, zi_ref, zt_ref, zh_ref, n_ref, ahead_ref, behind_ref, far_ref,
                 xi_ref, xt_ref, dui_ref, dut_ref, kept_ref, given_ref):
    scale = sb_ref[0]
    bias = sb_ref[1]
    zi = zi_ref[...]
    zt = zt_ref[...]
    rows = zi.shape[0]
    own = lax.broadcasted_iota(jnp.int32, (rows, rows), 0) == lax.broadcasted_iota(jnp.int32, (rows, rows), 1)

    def gate(cosine, mine):
        logit = scale * cosine + bias
        v = jnp.where(own, -logit, logit) if mine else logit
        e = jnp.exp(-jnp.abs(v))
        inv = 1.0 / (1.0 + e)
        dlogit = jnp.where(v >= 0, inv, e * inv)
        if mine:
            dlogit = jnp.where(own, -dlogit, dlogit)
        return v, e, dlogit

    def fold(x):
        return jnp.sum(x.reshape(rows // 8, 8, rows), axis=0)

    loss = gscale = gbias = None
    dz_img = dz_txt = None
    images, texts = slice(0, rows), slice(rows, 2 * rows)
    piece = rows // SPREAD

    def part(ref, at):
        return ref[:, at * piece : (at + 1) * piece, :].reshape(rows, zi.shape[1])

    pairs = (
        (lambda: zt, lambda: zi),
        (lambda: part(ahead_ref, 1), lambda: part(behind_ref, 0)),
        (lambda: part(behind_ref, 1), lambda: part(ahead_ref, 0)),
        (lambda: part(far_ref, 0), lambda: part(far_ref, 1)),
        (lambda: part(far_ref, 2), lambda: part(far_ref, 3)),
    )
    for k, (get_txt, get_img) in enumerate(pairs):
        txt = get_txt()
        cosine = dot_t(zi, txt)
        v, e, dlogit = gate(cosine, k == 0)
        parts = fold(jnp.maximum(v, 0.0) + jnp.log1p(e)), fold(dlogit * cosine), fold(dlogit)
        coef = (scale * dlogit).astype(jnp.bfloat16)
        to_img = jnp.dot(coef, txt, preferred_element_type=jnp.float32)
        img = get_img()
        if k == 0:
            coef_back = coef.T
        else:
            coef_back = (scale * gate(dot_t(zt, img), False)[2]).astype(jnp.bfloat16)
        to_txt = jnp.dot(coef_back, img, preferred_element_type=jnp.float32)
        if k == 0:
            loss, gscale, gbias = parts
            dz_img, dz_txt = to_img, to_txt
        else:
            loss, gscale, gbias = loss + parts[0], gscale + parts[1], gbias + parts[2]
            dz_img, dz_txt = dz_img + to_img, dz_txt + to_txt

    for dz, at, du_ref in ((dz_img, images, dui_ref), (dz_txt, texts, dut_ref)):
        zh = zh_ref[at, :]
        inner = jnp.sum(zh * dz, axis=-1, keepdims=True)
        du_ref[...] = ((dz - zh * inner) / n_ref[at, :]).astype(jnp.bfloat16)

    def head_grad(out_ref, x_ref, du_ref):
        width = x_ref.shape[1]
        out_ref[0:width, :] = lax.dot_general(
            x_ref[...], du_ref[...], (((0,), (0,)), ((), ())), preferred_element_type=jnp.float32
        )

    core = core_ref[0]

    @pl.when(core == 0)
    def _():
        head_grad(given_ref, xt_ref, dut_ref)
        head_grad(kept_ref, xi_ref, dui_ref)

    @pl.when(core == 1)
    def _():
        head_grad(given_ref, xi_ref, dui_ref)
        head_grad(kept_ref, xt_ref, dut_ref)

    at = lax.broadcasted_iota(jnp.int32, (8, kept_ref.shape[1]), 1)
    stats = jnp.where(at == 0, jnp.sum(loss), jnp.where(at == 1, jnp.sum(gscale), jnp.sum(gbias)))
    stats = jnp.where(at < 3, stats, 0.0)
    last = slice(kept_ref.shape[0] - 8, kept_ref.shape[0])
    kept_ref[last, :] = stats
    given_ref[last, :] = stats


def tiles(sb, core, z_img, z_txt, *others):
    rows, width = z_img.shape
    vmem = pl.BlockSpec(memory_space=pltpu.VMEM)
    return pl.pallas_call(
        tiles_kernel,
        out_shape=(
            jax.ShapeDtypeStruct((rows, width), jnp.bfloat16),
            jax.ShapeDtypeStruct((rows, width), jnp.bfloat16),
            jax.ShapeDtypeStruct((width + 8, width), jnp.float32),
            jax.ShapeDtypeStruct((width + 8, width), jnp.float32),
        ),
        in_specs=[pl.BlockSpec(memory_space=pltpu.SMEM)] * 2 + [vmem] * (2 + len(others)),
        out_specs=(vmem, vmem, vmem, vmem),
        compiler_params=pltpu.CompilerParams(vmem_limit_bytes=40 * 1024 * 1024),
        name="tiles",
    )(sb, core, z_img, z_txt, *others)


def summed_heads(given, kept, total):
    width = kept.shape[1]
    rows = width // (X * Y)
    both = kept + other_core(given)
    part = both[:width].astype(jnp.bfloat16)
    stats = both[width, 0:3]
    one = lax.reduce_precision(stats, 8, 7)
    two = lax.reduce_precision(stats - one, 8, 7)
    three = stats - one - two
    terms = jnp.stack([one, two, three])
    extra = jnp.zeros((8, width), jnp.bfloat16).at[0:3, 0:3].set(terms.astype(jnp.bfloat16))
    plane = jnp.concatenate([part.reshape(X * Y, rows, width), jnp.broadcast_to(extra[None], (X * Y, 8, width))], axis=1)
    plane = exchange(plane, PLANES)
    plane = jnp.sum(plane.astype(jnp.float32), axis=0)
    stats = jnp.sum(plane[rows : rows + 3, 0:3], axis=0)
    few = rows // Z
    extra = jnp.zeros((8 - few, width), jnp.float32).at[0, 0:3].set(stats)
    column = jnp.concatenate([plane[:rows].reshape(Z, few, width), jnp.broadcast_to(extra[None], (Z, 8 - few, width))], axis=1)
    column = jnp.sum(exchange(column, COLUMNS), axis=0) / total
    stats = column[few, 0:3]
    part = column[:few].astype(jnp.bfloat16)
    part = exchange(jnp.broadcast_to(part[None], (Z, few, width)), COLUMNS).reshape(rows, width)
    part = exchange(jnp.broadcast_to(part[None], (X * Y, rows, width)), PLANES).reshape(width, width)
    return part, stats


def local(image_feats, text_feats, image_head, text_head, logit_scale, logit_bias, round_offsets):
    total = float(COUNT * image_feats.shape[0])
    z_img, z_txt, both, zh, norms = embed(image_feats, text_feats, image_head, text_head)
    order = jnp.sort(round_offsets)
    ahead = shifted(both, -1)
    behind = shifted(both, 1)
    far = fetch(both, (order[1], order[2]))
    sb = jnp.concatenate([logit_scale, logit_bias])
    core = lax.axis_index("pairs") % CORES
    du_img, du_txt, kept, given = tiles(
        sb, core.reshape(1), z_img, z_txt, zh, norms, ahead, behind, far, image_feats, text_feats
    )
    part, sum_stats = summed_heads(given, kept, total)
    first = core == 0
    theirs = other_core(part)
    sum_wi = jnp.where(first, part, theirs).astype(jnp.float32)
    sum_wt = jnp.where(first, theirs, part).astype(jnp.float32)

    g_img = jnp.dot(du_img, image_head.T, preferred_element_type=jnp.float32).astype(jnp.bfloat16)
    g_txt = jnp.dot(du_txt, text_head.T, preferred_element_type=jnp.float32).astype(jnp.bfloat16)
    return (g_img, g_txt, sum_wi, sum_wt, sum_stats)


def solution(mesh):
    placed = (P("pairs", None), P("pairs", None), P(), P(), P(), P(), P())
    return jax.shard_map(
        local,
        mesh=mesh,
        in_specs=placed,
        out_specs=(P("pairs", None), P("pairs", None), P(), P(), P()),
        check_vma=False,
    )
```

```python
import jax
import jax.numpy as jnp
from jax import lax
from jax.experimental import pallas as pl
from jax.experimental.pallas import tpu as pltpu
from jax.sharding import PartitionSpec as P

EPS = 1e-06
X, Y, Z, CORES = 4, 4, 8, 2
COUNT = X * Y * Z * CORES
STEP = Z * CORES
SPREAD = X * Y

PLANES = [[xy * STEP + zc for xy in range(X * Y)] for zc in range(STEP)]
COLUMNS = [[xy * STEP + z * CORES + c for z in range(Z)] for xy in range(X * Y) for c in range(CORES)]


def shifted(value, steps):
    return lax.ppermute(value, "pairs", [(source, (source + steps) % COUNT) for source in range(COUNT)])


def other_core(value):
    return lax.ppermute(value, "pairs", [(source, source ^ 1) for source in range(COUNT)])


def exchange(value, groups):
    return lax.all_to_all(value, "pairs", 0, 0, axis_index_groups=groups, tiled=True)


def embed_kernel(xi_hbm, xt_hbm, wi_hbm, wt_hbm, both_ref, u_ref, x_ref, w_ref, sems):
    rows, width = xi_hbm.shape
    piece = both_ref.shape[1] // 2
    copies = []
    for k, (x_hbm, w_hbm) in enumerate(((xi_hbm, wi_hbm), (xt_hbm, wt_hbm))):
        copies.append(pltpu.make_async_copy(x_hbm, x_ref.at[k], sems.at[k, 0]))
        copies.append(pltpu.make_async_copy(w_hbm, w_ref.at[k], sems.at[k, 1]))
    for copy in copies:
        copy.start()
    for k in range(2):
        copies[2 * k].wait()
        copies[2 * k + 1].wait()
        proj = jnp.dot(x_ref[k], w_ref[k], preferred_element_type=jnp.float32)
        norms = jnp.sqrt(jnp.sum(proj * proj, axis=-1, keepdims=True) + EPS)
        z = (proj / norms).astype(jnp.bfloat16)
        u_ref[k * rows : (k + 1) * rows, :] = proj
        both_ref[:, k * piece : (k + 1) * piece, :] = z.reshape(SPREAD, piece, width)


def embed(image_feats, text_feats, image_head, text_head):
    rows, width = image_feats.shape
    vmem = pl.BlockSpec(memory_space=pltpu.VMEM)
    return pl.pallas_call(
        embed_kernel,
        out_shape=(
            jax.ShapeDtypeStruct((SPREAD, 2 * rows // SPREAD, width), jnp.bfloat16),
            jax.ShapeDtypeStruct((2 * rows, width), jnp.float32),
        ),
        in_specs=[pl.BlockSpec(memory_space=pl.ANY)] * 4,
        out_specs=(vmem,) * 2,
        scratch_shapes=[
            pltpu.VMEM((2, rows, width), jnp.bfloat16),
            pltpu.VMEM((2, width, width), jnp.bfloat16),
            pltpu.SemaphoreType.DMA((2, 2)),
        ],
        compiler_params=pltpu.CompilerParams(vmem_limit_bytes=60 * 1024 * 1024),
        name="embed",
    )(image_feats, text_feats, image_head, text_head)


def turned(value, steps):
    pairs = [(source, source // STEP * STEP + (source + steps) % STEP) for source in range(COUNT)]
    return lax.ppermute(value, "pairs", pairs)


def along(txt, img, low):
    def branch(steps):
        if steps == 0:
            return lambda txt, img: (txt, img)
        return lambda txt, img: (turned(txt, -steps), turned(img, steps))

    return tuple(lax.switch(low, [branch(k) for k in range(STEP)], txt, img))


def line_up_kernel(at_ref, a_ref, b_ref, c_ref, d_ref, out_ref):
    piece = a_ref.shape[1]
    for k, ref in enumerate((a_ref, b_ref, c_ref, d_ref)):
        for p in range(SPREAD):
            out_ref[p, k * piece : (k + 1) * piece, :] = ref[lax.rem(at_ref[k] + p, SPREAD)]


def line_up(at, parts):
    vmem = pl.BlockSpec(memory_space=pltpu.VMEM)
    slots, piece, width = parts[0].shape
    return pl.pallas_call(
        line_up_kernel,
        out_shape=jax.ShapeDtypeStruct((slots, len(parts) * piece, width), parts[0].dtype),
        in_specs=[pl.BlockSpec(memory_space=pltpu.SMEM)] + [vmem] * len(parts),
        out_specs=vmem,
        compiler_params=pltpu.CompilerParams(vmem_limit_bytes=16 * 1024 * 1024),
        name="line_up",
    )(at, *parts)


def fetch(both, offsets):
    piece = both.shape[1] // 2
    place = lax.axis_index("pairs") % STEP
    spread, ahead, behind = lax.optimization_barrier((exchange(both, PLANES), shifted(both, -1), shifted(both, 1)))
    img, txt = spread[:, :piece], spread[:, piece:]

    def turns(low):
        return jnp.minimum(jnp.mod(low, STEP), jnp.mod(-low, STEP))

    swap = turns(offsets[0]) > turns(offsets[1])
    one = jnp.where(swap, offsets[1], offsets[0])
    two = jnp.where(swap, offsets[0], offsets[1])
    one_txt, one_img = along(txt, img, jnp.mod(one, STEP))
    chain = turns(two - one) < turns(two)
    two_txt, two_img = along(
        jnp.where(chain, one_txt, txt),
        jnp.where(chain, one_img, img),
        jnp.mod(jnp.where(chain, two - one, two), STEP),
    )
    at = []
    for offset in (one, two):
        low, high = offset % STEP, offset // STEP
        at += [jnp.mod(high + (place + low) // STEP, SPREAD), jnp.mod(SPREAD - high - (place < low), SPREAD)]
    far = line_up(jnp.stack(at).astype(jnp.int32), (one_txt, one_img, two_txt, two_img))
    return ahead, behind, exchange(far, PLANES)


def dot_t(left, right):
    return lax.dot_general(left, right, (((1,), (1,)), ((), ())), preferred_element_type=jnp.float32)


def piece_of(ref, k, count=2):
    slots, rows, width = ref.shape
    rows = rows // count
    return ref[:, k * rows : (k + 1) * rows, :].reshape(slots * rows, width)


def fold(x):
    return jnp.sum(x.reshape(x.shape[0] // 8, 8, x.shape[1]), axis=0)


def gate(sb_ref, cosine, own):
    logit = sb_ref[0] * cosine + sb_ref[1]
    v = logit if own is None else jnp.where(own, -logit, logit)
    e = jnp.exp(-jnp.abs(v))
    inv = 1.0 / (1.0 + e)
    dlogit = jnp.where(v >= 0, inv, e * inv)
    if own is not None:
        dlogit = jnp.where(own, -dlogit, dlogit)
    return jnp.maximum(v, 0.0) + jnp.log1p(e), dlogit


def tile_pair(sb_ref, zi, zt, txt, img, own=None):
    cosine = dot_t(zi, txt)
    loss, dlogit = gate(sb_ref, cosine, own)
    coef = (sb_ref[0] * dlogit).astype(jnp.bfloat16)
    if own is None:
        coef_back = (sb_ref[0] * gate(sb_ref, dot_t(zt, img), None)[1]).astype(jnp.bfloat16)
    else:
        coef_back = coef.T
    to_img = jnp.dot(coef, txt, preferred_element_type=jnp.float32)
    to_txt = jnp.dot(coef_back, img, preferred_element_type=jnp.float32)
    return to_img, to_txt, fold(loss), fold(dlogit * cosine), fold(dlogit)


def added(left, right):
    return [a + b for a, b in zip(left, right)]


def near_kernel(sb_ref, both_ref, ahead_ref, behind_ref, dz_ref, stats_ref):
    zi, zt = piece_of(both_ref, 0), piece_of(both_ref, 1)
    rows = zi.shape[0]
    own = lax.broadcasted_iota(jnp.int32, (rows, rows), 0) == lax.broadcasted_iota(jnp.int32, (rows, rows), 1)
    sums = tile_pair(sb_ref, zi, zt, zt, zi, own)
    sums = added(sums, tile_pair(sb_ref, zi, zt, piece_of(ahead_ref, 1), piece_of(behind_ref, 0)))
    sums = added(sums, tile_pair(sb_ref, zi, zt, piece_of(behind_ref, 1), piece_of(ahead_ref, 0)))
    for k in range(2):
        dz_ref[k] = sums[k]
    for k in range(3):
        stats_ref[k] = sums[2 + k]


def near(sb, *arrays):
    slots, rows, width = arrays[0].shape
    rows = slots * rows // 2
    vmem = pl.BlockSpec(memory_space=pltpu.VMEM)
    return pl.pallas_call(
        near_kernel,
        out_shape=(
            jax.ShapeDtypeStruct((2, rows, width), jnp.float32),
            jax.ShapeDtypeStruct((3, 8, rows), jnp.float32),
        ),
        in_specs=[pl.BlockSpec(memory_space=pltpu.SMEM)] + [vmem] * len(arrays),
        out_specs=(vmem, vmem),
        compiler_params=pltpu.CompilerParams(vmem_limit_bytes=32 * 1024 * 1024),
        cost_estimate=pl.CostEstimate(flops=30 * rows * rows * width, bytes_accessed=8 * rows * width * 2, transcendentals=0),
        name="near",
    )(sb, *arrays)


def last_kernel(sb_ref, core_ref, both_ref, far_ref, dz_ref, stats_ref, u_hbm, xi_hbm, xt_hbm,
                dui_ref, dut_ref, kept_ref, given_ref, u_ref, x_ref, sems):
    copies = [
        pltpu.make_async_copy(u_hbm, u_ref, sems.at[0]),
        pltpu.make_async_copy(xi_hbm, x_ref.at[0], sems.at[1]),
        pltpu.make_async_copy(xt_hbm, x_ref.at[1], sems.at[2]),
    ]
    for copy in copies:
        copy.start()
    zi, zt = piece_of(both_ref, 0), piece_of(both_ref, 1)
    rows, width = zi.shape
    sums = tile_pair(sb_ref, zi, zt, piece_of(far_ref, 0, 4), piece_of(far_ref, 1, 4))
    sums = added(sums, tile_pair(sb_ref, zi, zt, piece_of(far_ref, 2, 4), piece_of(far_ref, 3, 4)))
    copies[0].wait()
    for k, du_ref in enumerate((dui_ref, dut_ref)):
        dz = dz_ref[k] + sums[k]
        proj = u_ref[k * rows : (k + 1) * rows, :]
        norms = jnp.sqrt(jnp.sum(proj * proj, axis=-1, keepdims=True) + EPS)
        zh = proj / norms
        inner = jnp.sum(zh * dz, axis=-1, keepdims=True)
        du_ref[...] = ((dz - zh * inner) / norms).astype(jnp.bfloat16)
    copies[1].wait()
    copies[2].wait()

    def head_grad(out_ref, x, du_ref):
        out_ref[0:width, :] = lax.dot_general(
            x, du_ref[...], (((0,), (0,)), ((), ())), preferred_element_type=jnp.float32
        ).astype(out_ref.dtype)

    core = core_ref[0]

    @pl.when(core == 0)
    def _():
        head_grad(given_ref, x_ref[1], dut_ref)
        head_grad(kept_ref, x_ref[0], dui_ref)

    @pl.when(core == 1)
    def _():
        head_grad(given_ref, x_ref[0], dui_ref)
        head_grad(kept_ref, x_ref[1], dut_ref)

    loss, gscale, gbias = (jnp.sum(stats_ref[k] + sums[2 + k]) for k in range(3))
    row = lax.broadcasted_iota(jnp.int32, (16, width), 0)
    at = lax.broadcasted_iota(jnp.int32, (16, width), 1)
    stats = jnp.where(at == 0, loss, jnp.where(at == 1, gscale, gbias))
    stats = jnp.where(at < 3, stats, 0.0)
    kept_ref[width : width + 8, :] = stats[0:8]
    one = stats.astype(jnp.bfloat16).astype(jnp.float32)
    two = (stats - one).astype(jnp.bfloat16).astype(jnp.float32)
    terms = jnp.where(row == 0, one, jnp.where(row == 1, two, jnp.where(row == 2, stats - one - two, 0.0)))
    given_ref[width : width + 16, :] = terms.astype(jnp.bfloat16)


def last(sb, core, both, far, dz, stats, u, image_feats, text_feats):
    rows, width = image_feats.shape
    vmem = pl.BlockSpec(memory_space=pltpu.VMEM)
    return pl.pallas_call(
        last_kernel,
        out_shape=(
            jax.ShapeDtypeStruct((rows, width), jnp.bfloat16),
            jax.ShapeDtypeStruct((rows, width), jnp.bfloat16),
            jax.ShapeDtypeStruct((width + 8, width), jnp.float32),
            jax.ShapeDtypeStruct((width + 16, width), jnp.bfloat16),
        ),
        in_specs=[pl.BlockSpec(memory_space=pltpu.SMEM)] * 2 + [vmem] * 4 + [pl.BlockSpec(memory_space=pl.ANY)] * 3,
        out_specs=(vmem,) * 4,
        scratch_shapes=[
            pltpu.VMEM((2 * rows, width), jnp.float32),
            pltpu.VMEM((2, rows, width), jnp.bfloat16),
            pltpu.SemaphoreType.DMA((3,)),
        ],
        compiler_params=pltpu.CompilerParams(vmem_limit_bytes=40 * 1024 * 1024),
        name="last",
    )(sb, core, both, far, dz, stats, u, image_feats, text_feats)


def summed_heads(given, kept, total):
    width = kept.shape[1]
    rows = width // (X * Y)
    got = other_core(given).astype(jnp.float32)
    part = (kept[:width] + got[:width]).astype(jnp.bfloat16)
    stats = kept[width, 0:3] + jnp.sum(got[width : width + 3, 0:3], axis=0)
    one = lax.reduce_precision(stats, 8, 7)
    two = lax.reduce_precision(stats - one, 8, 7)
    three = stats - one - two
    terms = jnp.stack([one, two, three])
    extra = jnp.zeros((8, width), jnp.bfloat16).at[0:3, 0:3].set(terms.astype(jnp.bfloat16))
    plane = jnp.concatenate([part.reshape(X * Y, rows, width), jnp.broadcast_to(extra[None], (X * Y, 8, width))], axis=1)
    plane = exchange(plane, PLANES)
    plane = jnp.sum(plane.astype(jnp.float32), axis=0)
    stats = jnp.sum(plane[rows : rows + 3, 0:3], axis=0)
    few = rows // Z
    extra = jnp.zeros((8 - few, width), jnp.float32).at[0, 0:3].set(stats)
    column = jnp.concatenate([plane[:rows].reshape(Z, few, width), jnp.broadcast_to(extra[None], (Z, 8 - few, width))], axis=1)
    column = jnp.sum(exchange(column, COLUMNS), axis=0) / total
    stats = column[few, 0:3]
    part = column[:few].astype(jnp.bfloat16)
    part = exchange(jnp.broadcast_to(part[None], (Z, few, width)), COLUMNS).reshape(rows, width)
    part = exchange(jnp.broadcast_to(part[None], (X * Y, rows, width)), PLANES).reshape(width, width)
    return part, stats


def local(image_feats, text_feats, image_head, text_head, logit_scale, logit_bias, round_offsets):
    total = float(COUNT * image_feats.shape[0])
    both, u = embed(image_feats, text_feats, image_head, text_head)
    order = jnp.sort(round_offsets)
    ahead, behind, far = fetch(both, (order[1], order[2]))
    sb = jnp.concatenate([logit_scale, logit_bias])
    core = lax.axis_index("pairs") % CORES
    dz, stats = near(sb, both, ahead, behind)
    du_img, du_txt, kept, given = last(sb, core.reshape(1), both, far, dz, stats, u, image_feats, text_feats)
    part, sum_stats = summed_heads(given, kept, total)
    first = core == 0
    theirs = other_core(part)
    sum_wi = jnp.where(first, part, theirs).astype(jnp.float32)
    sum_wt = jnp.where(first, theirs, part).astype(jnp.float32)

    g_img = jnp.dot(du_img, image_head.T, preferred_element_type=jnp.float32).astype(jnp.bfloat16)
    g_txt = jnp.dot(du_txt, text_head.T, preferred_element_type=jnp.float32).astype(jnp.bfloat16)
    return (g_img, g_txt, sum_wi, sum_wt, sum_stats)


def solution(mesh):
    placed = (P("pairs", None), P("pairs", None), P(), P(), P(), P(), P())
    return jax.shard_map(
        local,
        mesh=mesh,
        in_specs=placed,
        out_specs=(P("pairs", None), P("pairs", None), P(), P(), P()),
        check_vma=False,
    )
```

```python
import jax
import jax.numpy as jnp
from jax import lax
from jax.experimental import pallas as pl
from jax.experimental.pallas import tpu as pltpu
from jax.sharding import PartitionSpec as P

EPS = 1e-06
X, Y, Z, CORES = 4, 4, 8, 2
COUNT = X * Y * Z * CORES
STEP = Z * CORES
SPREAD = X * Y

PLANES = [[xy * STEP + zc for xy in range(X * Y)] for zc in range(STEP)]
COLUMNS = [[xy * STEP + z * CORES + c for z in range(Z)] for xy in range(X * Y) for c in range(CORES)]


def shifted(value, steps):
    return lax.ppermute(value, "pairs", [(source, (source + steps) % COUNT) for source in range(COUNT)])


def other_core(value):
    return lax.ppermute(value, "pairs", [(source, source ^ 1) for source in range(COUNT)])


def exchange(value, groups):
    return lax.all_to_all(value, "pairs", 0, 0, axis_index_groups=groups, tiled=True)


def embed_kernel(xi_hbm, xt_hbm, wi_hbm, wt_hbm, both_ref, u_ref, x_ref, w_ref, sems):
    rows, width = xi_hbm.shape
    piece = both_ref.shape[1] // 2
    copies = []
    for k, (x_hbm, w_hbm) in enumerate(((xi_hbm, wi_hbm), (xt_hbm, wt_hbm))):
        copies.append(pltpu.make_async_copy(x_hbm, x_ref.at[k], sems.at[k, 0]))
        copies.append(pltpu.make_async_copy(w_hbm, w_ref.at[k], sems.at[k, 1]))
    for copy in copies:
        copy.start()
    for k in range(2):
        copies[2 * k].wait()
        copies[2 * k + 1].wait()
        proj = jnp.dot(x_ref[k], w_ref[k], preferred_element_type=jnp.float32)
        norms = jnp.sqrt(jnp.sum(proj * proj, axis=-1, keepdims=True) + EPS)
        z = (proj / norms).astype(jnp.bfloat16)
        u_ref[k * rows : (k + 1) * rows, :] = proj
        both_ref[:, k * piece : (k + 1) * piece, :] = z.reshape(SPREAD, piece, width)


def embed(image_feats, text_feats, image_head, text_head):
    rows, width = image_feats.shape
    vmem = pl.BlockSpec(memory_space=pltpu.VMEM)
    return pl.pallas_call(
        embed_kernel,
        out_shape=(
            jax.ShapeDtypeStruct((SPREAD, 2 * rows // SPREAD, width), jnp.bfloat16),
            jax.ShapeDtypeStruct((2 * rows, width), jnp.float32),
        ),
        in_specs=[pl.BlockSpec(memory_space=pl.ANY)] * 4,
        out_specs=(vmem,) * 2,
        scratch_shapes=[
            pltpu.VMEM((2, rows, width), jnp.bfloat16),
            pltpu.VMEM((2, width, width), jnp.bfloat16),
            pltpu.SemaphoreType.DMA((2, 2)),
        ],
        compiler_params=pltpu.CompilerParams(vmem_limit_bytes=60 * 1024 * 1024),
        name="embed",
    )(image_feats, text_feats, image_head, text_head)


def turned(value, steps):
    pairs = [(source, source // STEP * STEP + (source + steps) % STEP) for source in range(COUNT)]
    return lax.ppermute(value, "pairs", pairs)


def along(txt, img, low):
    def branch(steps):
        if steps == 0:
            return lambda txt, img: (txt, img)
        return lambda txt, img: (turned(txt, -steps), turned(img, steps))

    return tuple(lax.switch(low, [branch(k) for k in range(STEP)], txt, img))


def line_up_kernel(at_ref, a_ref, b_ref, c_ref, d_ref, out_ref):
    piece = a_ref.shape[1]
    for k, ref in enumerate((a_ref, b_ref, c_ref, d_ref)):
        for p in range(SPREAD):
            out_ref[p, k * piece : (k + 1) * piece, :] = ref[lax.rem(at_ref[k] + p, SPREAD)]


def line_up(at, parts):
    vmem = pl.BlockSpec(memory_space=pltpu.VMEM)
    slots, piece, width = parts[0].shape
    return pl.pallas_call(
        line_up_kernel,
        out_shape=jax.ShapeDtypeStruct((slots, len(parts) * piece, width), parts[0].dtype),
        in_specs=[pl.BlockSpec(memory_space=pltpu.SMEM)] + [vmem] * len(parts),
        out_specs=vmem,
        compiler_params=pltpu.CompilerParams(vmem_limit_bytes=16 * 1024 * 1024),
        name="line_up",
    )(at, *parts)


def fetch(both, offsets):
    piece = both.shape[1] // 2
    place = lax.axis_index("pairs") % STEP
    spread, ahead, behind = lax.optimization_barrier((exchange(both, PLANES), shifted(both, -1), shifted(both, 1)))
    img, txt = spread[:, :piece], spread[:, piece:]

    def turns(low):
        return jnp.minimum(jnp.mod(low, STEP), jnp.mod(-low, STEP))

    swap = turns(offsets[0]) > turns(offsets[1])
    one = jnp.where(swap, offsets[1], offsets[0])
    two = jnp.where(swap, offsets[0], offsets[1])
    one_txt, one_img = along(txt, img, jnp.mod(one, STEP))
    chain = turns(two - one) < turns(two)
    two_txt, two_img = along(
        jnp.where(chain, one_txt, txt),
        jnp.where(chain, one_img, img),
        jnp.mod(jnp.where(chain, two - one, two), STEP),
    )
    at = []
    for offset in (one, two):
        low, high = offset % STEP, offset // STEP
        at += [jnp.mod(high + (place + low) // STEP, SPREAD), jnp.mod(SPREAD - high - (place < low), SPREAD)]
    far = line_up(jnp.stack(at).astype(jnp.int32), (one_txt, one_img, two_txt, two_img))
    return ahead, behind, exchange(far, PLANES)


def dot_t(left, right):
    return lax.dot_general(left, right, (((1,), (1,)), ((), ())), preferred_element_type=jnp.float32)


def piece_of(ref, k, count=2):
    slots, rows, width = ref.shape
    rows = rows // count
    return ref[:, k * rows : (k + 1) * rows, :].reshape(slots * rows, width)


def fold(x):
    return jnp.sum(x.reshape(x.shape[0] // 8, 8, x.shape[1]), axis=0)


def gate(sb_ref, cosine, own):
    logit = sb_ref[0] * cosine + sb_ref[1]
    v = logit if own is None else jnp.where(own, -logit, logit)
    e = jnp.exp(-jnp.abs(v))
    inv = 1.0 / (1.0 + e)
    dlogit = jnp.where(v >= 0, inv, e * inv)
    if own is not None:
        dlogit = jnp.where(own, -dlogit, dlogit)
    return jnp.maximum(v, 0.0) + jnp.log1p(e), dlogit


def tile_pair(sb_ref, zi, zt, txt, img, own=None):
    cosine = dot_t(zi, txt)
    loss, dlogit = gate(sb_ref, cosine, own)
    coef = (sb_ref[0] * dlogit).astype(jnp.bfloat16)
    if own is None:
        coef_back = (sb_ref[0] * gate(sb_ref, dot_t(zt, img), None)[1]).astype(jnp.bfloat16)
    else:
        coef_back = coef.T
    to_img = jnp.dot(coef, txt, preferred_element_type=jnp.float32)
    to_txt = jnp.dot(coef_back, img, preferred_element_type=jnp.float32)
    return to_img, to_txt, fold(loss), fold(dlogit * cosine), fold(dlogit)


def added(left, right):
    return [a + b for a, b in zip(left, right)]


def near_kernel(sb_ref, both_ref, ahead_ref, behind_ref, dz_ref, stats_ref):
    zi, zt = piece_of(both_ref, 0), piece_of(both_ref, 1)
    rows = zi.shape[0]
    own = lax.broadcasted_iota(jnp.int32, (rows, rows), 0) == lax.broadcasted_iota(jnp.int32, (rows, rows), 1)
    sums = tile_pair(sb_ref, zi, zt, zt, zi, own)
    sums = added(sums, tile_pair(sb_ref, zi, zt, piece_of(ahead_ref, 1), piece_of(behind_ref, 0)))
    sums = added(sums, tile_pair(sb_ref, zi, zt, piece_of(behind_ref, 1), piece_of(ahead_ref, 0)))
    for k in range(2):
        dz_ref[k] = sums[k]
    for k in range(3):
        stats_ref[k] = sums[2 + k]


def near(sb, *arrays):
    slots, rows, width = arrays[0].shape
    rows = slots * rows // 2
    vmem = pl.BlockSpec(memory_space=pltpu.VMEM)
    return pl.pallas_call(
        near_kernel,
        out_shape=(
            jax.ShapeDtypeStruct((2, rows, width), jnp.float32),
            jax.ShapeDtypeStruct((3, 8, rows), jnp.float32),
        ),
        in_specs=[pl.BlockSpec(memory_space=pltpu.SMEM)] + [vmem] * len(arrays),
        out_specs=(vmem, vmem),
        compiler_params=pltpu.CompilerParams(vmem_limit_bytes=32 * 1024 * 1024),
        cost_estimate=pl.CostEstimate(flops=30 * rows * rows * width, bytes_accessed=8 * rows * width * 2, transcendentals=0),
        name="near",
    )(sb, *arrays)


def last_kernel(sb_ref, core_ref, both_ref, far_ref, dz_ref, stats_ref, u_hbm, xi_hbm, xt_hbm,
                dui_ref, dut_ref, kept_ref, given_ref, u_ref, x_ref, sems):
    copies = [
        pltpu.make_async_copy(u_hbm, u_ref, sems.at[0]),
        pltpu.make_async_copy(xi_hbm, x_ref.at[0], sems.at[1]),
        pltpu.make_async_copy(xt_hbm, x_ref.at[1], sems.at[2]),
    ]
    for copy in copies:
        copy.start()
    zi, zt = piece_of(both_ref, 0), piece_of(both_ref, 1)
    rows, width = zi.shape
    sums = tile_pair(sb_ref, zi, zt, piece_of(far_ref, 0, 4), piece_of(far_ref, 1, 4))
    sums = added(sums, tile_pair(sb_ref, zi, zt, piece_of(far_ref, 2, 4), piece_of(far_ref, 3, 4)))
    copies[0].wait()
    for k, du_ref in enumerate((dui_ref, dut_ref)):
        dz = dz_ref[k] + sums[k]
        proj = u_ref[k * rows : (k + 1) * rows, :]
        norms = jnp.sqrt(jnp.sum(proj * proj, axis=-1, keepdims=True) + EPS)
        zh = proj / norms
        inner = jnp.sum(zh * dz, axis=-1, keepdims=True)
        du_ref[...] = ((dz - zh * inner) / norms).astype(jnp.bfloat16)
    copies[1].wait()
    copies[2].wait()

    def head_grad(out_ref, x, du_ref):
        out_ref[0:width, :] = lax.dot_general(
            x, du_ref[...], (((0,), (0,)), ((), ())), preferred_element_type=jnp.float32
        ).astype(out_ref.dtype)

    core = core_ref[0]

    @pl.when(core == 0)
    def _():
        head_grad(given_ref, x_ref[1], dut_ref)
        head_grad(kept_ref, x_ref[0], dui_ref)

    @pl.when(core == 1)
    def _():
        head_grad(given_ref, x_ref[0], dui_ref)
        head_grad(kept_ref, x_ref[1], dut_ref)

    loss, gscale, gbias = (jnp.sum(stats_ref[k] + sums[2 + k]) for k in range(3))
    row = lax.broadcasted_iota(jnp.int32, (16, width), 0)
    at = lax.broadcasted_iota(jnp.int32, (16, width), 1)
    stats = jnp.where(at == 0, loss, jnp.where(at == 1, gscale, gbias))
    stats = jnp.where(at < 3, stats, 0.0)
    kept_ref[width : width + 8, :] = stats[0:8]
    one = stats.astype(jnp.bfloat16).astype(jnp.float32)
    two = (stats - one).astype(jnp.bfloat16).astype(jnp.float32)
    terms = jnp.where(row == 0, one, jnp.where(row == 1, two, jnp.where(row == 2, stats - one - two, 0.0)))
    given_ref[width : width + 16, :] = terms.astype(jnp.bfloat16)


def last(sb, core, both, far, dz, stats, u, image_feats, text_feats):
    rows, width = image_feats.shape
    vmem = pl.BlockSpec(memory_space=pltpu.VMEM)
    return pl.pallas_call(
        last_kernel,
        out_shape=(
            jax.ShapeDtypeStruct((rows, width), jnp.bfloat16),
            jax.ShapeDtypeStruct((rows, width), jnp.bfloat16),
            jax.ShapeDtypeStruct((width + 8, width), jnp.float32),
            jax.ShapeDtypeStruct((width + 16, width), jnp.bfloat16),
        ),
        in_specs=[pl.BlockSpec(memory_space=pltpu.SMEM)] * 2 + [vmem] * 4 + [pl.BlockSpec(memory_space=pl.ANY)] * 3,
        out_specs=(vmem,) * 4,
        scratch_shapes=[
            pltpu.VMEM((2 * rows, width), jnp.float32),
            pltpu.VMEM((2, rows, width), jnp.bfloat16),
            pltpu.SemaphoreType.DMA((3,)),
        ],
        compiler_params=pltpu.CompilerParams(vmem_limit_bytes=40 * 1024 * 1024),
        name="last",
    )(sb, core, both, far, dz, stats, u, image_feats, text_feats)


def terms_of(stats):
    one = lax.reduce_precision(stats, 8, 7)
    two = lax.reduce_precision(stats - one, 8, 7)
    return jnp.concatenate([one, two, stats - one - two]).astype(jnp.bfloat16)


def summed_heads(given, kept, total):
    width = kept.shape[1]
    rows = width // (X * Y)
    got = other_core(given).astype(jnp.float32)
    part = (kept[:width] + got[:width]).astype(jnp.bfloat16)
    stats = kept[width, 0:3] + jnp.sum(got[width : width + 3, 0:3], axis=0)
    extra = jnp.zeros((8, width), jnp.bfloat16).at[0, 0:9].set(terms_of(stats))
    plane = jnp.concatenate([part.reshape(X * Y, rows, width), jnp.broadcast_to(extra[None], (X * Y, 8, width))], axis=1)
    plane = exchange(plane, PLANES)
    plane = jnp.sum(plane.astype(jnp.float32), axis=0)
    stats = jnp.sum(plane[rows, 0:9].reshape(3, 3), axis=0)
    few = rows // Z
    extra = jnp.zeros((8 - few, width), jnp.bfloat16).at[0, 0:9].set(terms_of(stats))
    part = plane[:rows].astype(jnp.bfloat16).reshape(Z, few, width)
    column = jnp.concatenate([part, jnp.broadcast_to(extra[None], (Z, 8 - few, width))], axis=1)
    column = jnp.sum(exchange(column, COLUMNS).astype(jnp.float32), axis=0) / total
    stats = jnp.sum(column[few, 0:9].reshape(3, 3), axis=0)
    part = column[:few].astype(jnp.bfloat16)
    part = exchange(jnp.broadcast_to(part[None], (Z, few, width)), COLUMNS).reshape(rows, width)
    part = exchange(jnp.broadcast_to(part[None], (X * Y, rows, width)), PLANES).reshape(width, width)
    return part, stats


def local(image_feats, text_feats, image_head, text_head, logit_scale, logit_bias, round_offsets):
    total = float(COUNT * image_feats.shape[0])
    both, u = embed(image_feats, text_feats, image_head, text_head)
    order = jnp.sort(round_offsets)
    ahead, behind, far = fetch(both, (order[1], order[2]))
    sb = jnp.concatenate([logit_scale, logit_bias])
    core = lax.axis_index("pairs") % CORES
    dz, stats = near(sb, both, ahead, behind)
    du_img, du_txt, kept, given = last(sb, core.reshape(1), both, far, dz, stats, u, image_feats, text_feats)
    part, sum_stats = summed_heads(given, kept, total)
    first = core == 0
    theirs = other_core(part)
    sum_wi = jnp.where(first, part, theirs).astype(jnp.float32)
    sum_wt = jnp.where(first, theirs, part).astype(jnp.float32)

    g_img = jnp.dot(du_img, image_head.T, preferred_element_type=jnp.float32).astype(jnp.bfloat16)
    g_txt = jnp.dot(du_txt, text_head.T, preferred_element_type=jnp.float32).astype(jnp.bfloat16)
    return (g_img, g_txt, sum_wi, sum_wt, sum_stats)


def solution(mesh):
    placed = (P("pairs", None), P("pairs", None), P(), P(), P(), P(), P())
    return jax.shard_map(
        local,
        mesh=mesh,
        in_specs=placed,
        out_specs=(P("pairs", None), P("pairs", None), P(), P(), P()),
        check_vma=False,
    )
```

```python
import functools

import jax
import jax.numpy as jnp
from jax import lax
from jax.experimental import pallas as pl
from jax.experimental.pallas import tpu as pltpu
from jax.sharding import PartitionSpec as P

EPS = 1e-06
X, Y, Z, CORES = 4, 4, 8, 2
COUNT = X * Y * Z * CORES
STEP = Z * CORES
SPREAD = X * Y

PLANES = [[xy * STEP + zc for xy in range(X * Y)] for zc in range(STEP)]
COLUMNS = [[xy * STEP + z * CORES + c for z in range(Z)] for xy in range(X * Y) for c in range(CORES)]


def shifted(value, steps):
    return lax.ppermute(value, "pairs", [(source, (source + steps) % COUNT) for source in range(COUNT)])


def other_core(value):
    return lax.ppermute(value, "pairs", [(source, source ^ 1) for source in range(COUNT)])


def exchange(value, groups):
    return lax.all_to_all(value, "pairs", 0, 0, axis_index_groups=groups, tiled=True)


def embed_kernel(xi_hbm, xt_hbm, wi_hbm, wt_hbm, both_ref, u_ref, x_ref, w_ref, sems):
    rows, width = xi_hbm.shape
    piece = both_ref.shape[1] // 2
    copies = []
    for k, (x_hbm, w_hbm) in enumerate(((xi_hbm, wi_hbm), (xt_hbm, wt_hbm))):
        copies.append(pltpu.make_async_copy(x_hbm, x_ref.at[k], sems.at[k, 0]))
        copies.append(pltpu.make_async_copy(w_hbm, w_ref.at[k], sems.at[k, 1]))
    for copy in copies:
        copy.start()
    for k in range(2):
        copies[2 * k].wait()
        copies[2 * k + 1].wait()
        proj = jnp.dot(x_ref[k], w_ref[k], preferred_element_type=jnp.float32)
        norms = jnp.sqrt(jnp.sum(proj * proj, axis=-1, keepdims=True) + EPS)
        z = (proj / norms).astype(jnp.bfloat16)
        u_ref[k * rows : (k + 1) * rows, :] = proj
        both_ref[:, k * piece : (k + 1) * piece, :] = z.reshape(SPREAD, piece, width)


def embed(image_feats, text_feats, image_head, text_head):
    rows, width = image_feats.shape
    vmem = pl.BlockSpec(memory_space=pltpu.VMEM)
    return pl.pallas_call(
        embed_kernel,
        out_shape=(
            jax.ShapeDtypeStruct((SPREAD, 2 * rows // SPREAD, width), jnp.bfloat16),
            jax.ShapeDtypeStruct((2 * rows, width), jnp.float32),
        ),
        in_specs=[pl.BlockSpec(memory_space=pl.ANY)] * 4,
        out_specs=(vmem,) * 2,
        scratch_shapes=[
            pltpu.VMEM((2, rows, width), jnp.bfloat16),
            pltpu.VMEM((2, width, width), jnp.bfloat16),
            pltpu.SemaphoreType.DMA((2, 2)),
        ],
        compiler_params=pltpu.CompilerParams(vmem_limit_bytes=60 * 1024 * 1024),
        name="embed",
    )(image_feats, text_feats, image_head, text_head)


def turned(value, steps):
    pairs = [(source, source // STEP * STEP + (source + steps) % STEP) for source in range(COUNT)]
    return lax.ppermute(value, "pairs", pairs)


def along(txt, img, low):
    def branch(steps):
        if steps == 0:
            return lambda txt, img: (txt, img)
        return lambda txt, img: (turned(txt, -steps), turned(img, steps))

    return tuple(lax.switch(low, [branch(k) for k in range(STEP)], txt, img))


def line_up_kernel(at_ref, a_ref, b_ref, c_ref, d_ref, out_ref):
    piece = a_ref.shape[1]
    for k, ref in enumerate((a_ref, b_ref, c_ref, d_ref)):
        for p in range(SPREAD):
            out_ref[p, k * piece : (k + 1) * piece, :] = ref[lax.rem(at_ref[k] + p, SPREAD)]


def line_up(at, parts):
    vmem = pl.BlockSpec(memory_space=pltpu.VMEM)
    slots, piece, width = parts[0].shape
    return pl.pallas_call(
        line_up_kernel,
        out_shape=jax.ShapeDtypeStruct((slots, len(parts) * piece, width), parts[0].dtype),
        in_specs=[pl.BlockSpec(memory_space=pltpu.SMEM)] + [vmem] * len(parts),
        out_specs=vmem,
        compiler_params=pltpu.CompilerParams(vmem_limit_bytes=16 * 1024 * 1024),
        name="line_up",
    )(at, *parts)


def fetch(both, offsets):
    piece = both.shape[1] // 2
    place = lax.axis_index("pairs") % STEP
    spread, ahead, behind = lax.optimization_barrier((exchange(both, PLANES), shifted(both, -1), shifted(both, 1)))
    img, txt = spread[:, :piece], spread[:, piece:]

    def turns(low):
        return jnp.minimum(jnp.mod(low, STEP), jnp.mod(-low, STEP))

    swap = turns(offsets[0]) > turns(offsets[1])
    one = jnp.where(swap, offsets[1], offsets[0])
    two = jnp.where(swap, offsets[0], offsets[1])
    one_txt, one_img = along(txt, img, jnp.mod(one, STEP))
    chain = turns(two - one) < turns(two)
    two_txt, two_img = along(
        jnp.where(chain, one_txt, txt),
        jnp.where(chain, one_img, img),
        jnp.mod(jnp.where(chain, two - one, two), STEP),
    )
    at = []
    for offset in (one, two):
        low, high = offset % STEP, offset // STEP
        at += [jnp.mod(high + (place + low) // STEP, SPREAD), jnp.mod(SPREAD - high - (place < low), SPREAD)]
    far = line_up(jnp.stack(at).astype(jnp.int32), (one_txt, one_img, two_txt, two_img))
    return ahead, behind, exchange(far, PLANES)


def dot_t(left, right):
    return lax.dot_general(left, right, (((1,), (1,)), ((), ())), preferred_element_type=jnp.float32)


def piece_of(ref, k, count=2):
    slots, rows, width = ref.shape
    rows = rows // count
    return ref[:, k * rows : (k + 1) * rows, :].reshape(slots * rows, width)


def fold(x):
    return jnp.sum(x.reshape(x.shape[0] // 8, 8, x.shape[1]), axis=0)


def gate(sb_ref, cosine, own):
    logit = sb_ref[0] * cosine + sb_ref[1]
    v = logit if own is None else jnp.where(own, -logit, logit)
    e = jnp.exp(-jnp.abs(v))
    inv = 1.0 / (1.0 + e)
    dlogit = jnp.where(v >= 0, inv, e * inv)
    if own is not None:
        dlogit = jnp.where(own, -dlogit, dlogit)
    return jnp.maximum(v, 0.0) + jnp.log1p(e), dlogit


def tile_pair(sb_ref, zi, zt, txt, img, own=None):
    cosine = dot_t(zi, txt)
    loss, dlogit = gate(sb_ref, cosine, own)
    coef = (sb_ref[0] * dlogit).astype(jnp.bfloat16)
    if own is None:
        coef_back = (sb_ref[0] * gate(sb_ref, dot_t(zt, img), None)[1]).astype(jnp.bfloat16)
    else:
        coef_back = coef.T
    to_img = jnp.dot(coef, txt, preferred_element_type=jnp.float32)
    to_txt = jnp.dot(coef_back, img, preferred_element_type=jnp.float32)
    return to_img, to_txt, fold(loss), fold(dlogit * cosine), fold(dlogit)


def added(left, right):
    return [a + b for a, b in zip(left, right)]


def near_kernel(sb_ref, both_ref, ahead_ref, behind_ref, dz_ref, stats_ref):
    zi, zt = piece_of(both_ref, 0), piece_of(both_ref, 1)
    rows = zi.shape[0]
    own = lax.broadcasted_iota(jnp.int32, (rows, rows), 0) == lax.broadcasted_iota(jnp.int32, (rows, rows), 1)
    sums = tile_pair(sb_ref, zi, zt, zt, zi, own)
    sums = added(sums, tile_pair(sb_ref, zi, zt, piece_of(ahead_ref, 1), piece_of(behind_ref, 0)))
    sums = added(sums, tile_pair(sb_ref, zi, zt, piece_of(behind_ref, 1), piece_of(ahead_ref, 0)))
    for k in range(2):
        dz_ref[k] = sums[k]
    for k in range(3):
        stats_ref[k] = sums[2 + k]


def near(sb, *arrays):
    slots, rows, width = arrays[0].shape
    rows = slots * rows // 2
    vmem = pl.BlockSpec(memory_space=pltpu.VMEM)
    return pl.pallas_call(
        near_kernel,
        out_shape=(
            jax.ShapeDtypeStruct((2, rows, width), jnp.float32),
            jax.ShapeDtypeStruct((3, 8, rows), jnp.float32),
        ),
        in_specs=[pl.BlockSpec(memory_space=pltpu.SMEM)] + [vmem] * len(arrays),
        out_specs=(vmem, vmem),
        compiler_params=pltpu.CompilerParams(vmem_limit_bytes=32 * 1024 * 1024),
        cost_estimate=pl.CostEstimate(flops=30 * rows * rows * width, bytes_accessed=8 * rows * width * 2, transcendentals=0),
        name="near",
    )(sb, *arrays)


def last_kernel(sb_ref, core_ref, both_ref, far_ref, dz_ref, stats_ref, u_hbm, xi_hbm, xt_hbm,
                dui_ref, dut_ref, kept_ref, given_ref, u_ref, x_ref, sems):
    copies = [
        pltpu.make_async_copy(u_hbm, u_ref, sems.at[0]),
        pltpu.make_async_copy(xi_hbm, x_ref.at[0], sems.at[1]),
        pltpu.make_async_copy(xt_hbm, x_ref.at[1], sems.at[2]),
    ]
    for copy in copies:
        copy.start()
    zi, zt = piece_of(both_ref, 0), piece_of(both_ref, 1)
    rows, width = zi.shape
    sums = tile_pair(sb_ref, zi, zt, piece_of(far_ref, 0, 4), piece_of(far_ref, 1, 4))
    sums = added(sums, tile_pair(sb_ref, zi, zt, piece_of(far_ref, 2, 4), piece_of(far_ref, 3, 4)))
    copies[0].wait()
    for k, du_ref in enumerate((dui_ref, dut_ref)):
        dz = dz_ref[k] + sums[k]
        proj = u_ref[k * rows : (k + 1) * rows, :]
        norms = jnp.sqrt(jnp.sum(proj * proj, axis=-1, keepdims=True) + EPS)
        zh = proj / norms
        inner = jnp.sum(zh * dz, axis=-1, keepdims=True)
        du_ref[...] = ((dz - zh * inner) / norms).astype(jnp.bfloat16)
    copies[1].wait()
    copies[2].wait()

    def head_grad(out_ref, x, du_ref):
        out_ref[0:width, :] = lax.dot_general(
            x, du_ref[...], (((0,), (0,)), ((), ())), preferred_element_type=jnp.float32
        ).astype(out_ref.dtype)

    core = core_ref[0]

    @pl.when(core == 0)
    def _():
        head_grad(given_ref, x_ref[1], dut_ref)
        head_grad(kept_ref, x_ref[0], dui_ref)

    @pl.when(core == 1)
    def _():
        head_grad(given_ref, x_ref[0], dui_ref)
        head_grad(kept_ref, x_ref[1], dut_ref)

    loss, gscale, gbias = (jnp.sum(stats_ref[k] + sums[2 + k]) for k in range(3))
    row = lax.broadcasted_iota(jnp.int32, (16, width), 0)
    at = lax.broadcasted_iota(jnp.int32, (16, width), 1)
    stats = jnp.where(at == 0, loss, jnp.where(at == 1, gscale, gbias))
    stats = jnp.where(at < 3, stats, 0.0)
    kept_ref[width : width + 8, :] = stats[0:8]
    one = stats.astype(jnp.bfloat16).astype(jnp.float32)
    two = (stats - one).astype(jnp.bfloat16).astype(jnp.float32)
    terms = jnp.where(row == 0, one, jnp.where(row == 1, two, jnp.where(row == 2, stats - one - two, 0.0)))
    given_ref[width : width + 16, :] = terms.astype(jnp.bfloat16)


def last(sb, core, both, far, dz, stats, u, image_feats, text_feats):
    rows, width = image_feats.shape
    vmem = pl.BlockSpec(memory_space=pltpu.VMEM)
    return pl.pallas_call(
        last_kernel,
        out_shape=(
            jax.ShapeDtypeStruct((rows, width), jnp.bfloat16),
            jax.ShapeDtypeStruct((rows, width), jnp.bfloat16),
            jax.ShapeDtypeStruct((width + 8, width), jnp.float32),
            jax.ShapeDtypeStruct((width + 16, width), jnp.bfloat16),
        ),
        in_specs=[pl.BlockSpec(memory_space=pltpu.SMEM)] * 2 + [vmem] * 4 + [pl.BlockSpec(memory_space=pl.ANY)] * 3,
        out_specs=(vmem,) * 4,
        scratch_shapes=[
            pltpu.VMEM((2 * rows, width), jnp.float32),
            pltpu.VMEM((2, rows, width), jnp.bfloat16),
            pltpu.SemaphoreType.DMA((3,)),
        ],
        compiler_params=pltpu.CompilerParams(vmem_limit_bytes=40 * 1024 * 1024),
        name="last",
    )(sb, core, both, far, dz, stats, u, image_feats, text_feats)


def terms_of(stats):
    one = lax.reduce_precision(stats, 8, 7)
    two = lax.reduce_precision(stats - one, 8, 7)
    return jnp.concatenate([one, two, stats - one - two]).astype(jnp.bfloat16)


def summed_heads(got, kept, total):
    width = kept.shape[1]
    rows = width // (X * Y)
    part = (kept[:width] + got[:width].astype(jnp.float32)).astype(jnp.bfloat16)
    stats = kept[width, 0:3] + jnp.sum(got[width : width + 3, 0:3].astype(jnp.float32), axis=0)
    extra = jnp.zeros((8, width), jnp.bfloat16).at[0, 0:9].set(terms_of(stats))
    plane = jnp.concatenate([part.reshape(X * Y, rows, width), jnp.broadcast_to(extra[None], (X * Y, 8, width))], axis=1)
    plane = exchange(plane, PLANES)
    plane = jnp.sum(plane.astype(jnp.float32), axis=0)
    stats = jnp.sum(plane[rows, 0:9].reshape(3, 3), axis=0)
    few = rows // Z
    extra = jnp.zeros((8 - few, width), jnp.bfloat16).at[0, 0:9].set(terms_of(stats))
    part = plane[:rows].astype(jnp.bfloat16).reshape(Z, few, width)
    column = jnp.concatenate([part, jnp.broadcast_to(extra[None], (Z, 8 - few, width))], axis=1)
    column = jnp.sum(exchange(column, COLUMNS).astype(jnp.float32), axis=0) / total
    stats = jnp.sum(column[few, 0:9].reshape(3, 3), axis=0)
    part = column[:few].astype(jnp.bfloat16)
    part = exchange(jnp.broadcast_to(part[None], (Z, few, width)), COLUMNS).reshape(rows, width)
    part = exchange(jnp.broadcast_to(part[None], (X * Y, rows, width)), PLANES).reshape(width, width)
    return part, stats


def write_kernel(turn, core_ref, part_ref, *refs):
    img_hbm, txt_hbm, wide_ref, sems = refs[-4:]
    rows = part_ref.shape[0] // sems.shape[0]

    def write(out_hbm):
        copies = []
        for k in range(sems.shape[0]):
            at = slice(k * rows, (k + 1) * rows)
            wide_ref[at, :] = part_ref[at, :].astype(jnp.float32)
            copies.append(pltpu.make_async_copy(wide_ref.at[at, :], out_hbm.at[at, :], sems.at[k]))
            copies[-1].start()
        for copy in copies:
            copy.wait()

    @pl.when(core_ref[0] == turn)
    def _():
        write(img_hbm)

    @pl.when(core_ref[0] != turn)
    def _():
        write(txt_hbm)


def write_head(turn, core, part, outs=()):
    width = part.shape[1]
    hbm = pl.BlockSpec(memory_space=pl.ANY)
    return pl.pallas_call(
        functools.partial(write_kernel, turn),
        out_shape=(jax.ShapeDtypeStruct(part.shape, jnp.float32),) * 2,
        in_specs=[pl.BlockSpec(memory_space=pltpu.SMEM), pl.BlockSpec(memory_space=pltpu.VMEM)] + [hbm] * len(outs),
        out_specs=(hbm, hbm),
        scratch_shapes=[pltpu.VMEM(part.shape, jnp.float32), pltpu.SemaphoreType.DMA((8,))],
        input_output_aliases={2 + k: k for k in range(len(outs))},
        compiler_params=pltpu.CompilerParams(vmem_limit_bytes=16 * 1024 * 1024),
        cost_estimate=pl.CostEstimate(flops=width * width, bytes_accessed=6 * width * width, transcendentals=0),
        name="write_head",
    )(core, part, *outs)


def local(image_feats, text_feats, image_head, text_head, logit_scale, logit_bias, round_offsets):
    total = float(COUNT * image_feats.shape[0])
    both, u = embed(image_feats, text_feats, image_head, text_head)
    order = jnp.sort(round_offsets)
    ahead, behind, far = fetch(both, (order[1], order[2]))
    sb = jnp.concatenate([logit_scale, logit_bias])
    core = lax.axis_index("pairs") % CORES
    dz, stats = near(sb, both, ahead, behind)
    du_img, du_txt, kept, given = last(sb, core.reshape(1), both, far, dz, stats, u, image_feats, text_feats)
    g_img = jnp.dot(du_img, image_head.T, preferred_element_type=jnp.float32).astype(jnp.bfloat16)
    g_txt = jnp.dot(du_txt, text_head.T, preferred_element_type=jnp.float32).astype(jnp.bfloat16)
    got, g_img, g_txt = lax.optimization_barrier((other_core(given), g_img, g_txt))
    part, sum_stats = summed_heads(got, kept, total)
    theirs, outs = lax.optimization_barrier((other_core(part), write_head(0, core.reshape(1), part)))
    sum_wi, sum_wt = write_head(1, core.reshape(1), theirs, outs)
    return (g_img, g_txt, sum_wi, sum_wt, sum_stats)


def solution(mesh):
    placed = (P("pairs", None), P("pairs", None), P(), P(), P(), P(), P())
    return jax.shard_map(
        local,
        mesh=mesh,
        in_specs=placed,
        out_specs=(P("pairs", None), P("pairs", None), P(), P(), P()),
        check_vma=False,
    )
```

```python
import functools

import jax
import jax.numpy as jnp
from jax import lax
from jax.experimental import pallas as pl
from jax.experimental.pallas import tpu as pltpu
from jax.sharding import PartitionSpec as P

EPS = 1e-06
X, Y, Z, CORES = 4, 4, 8, 2
COUNT = X * Y * Z * CORES
STEP = Z * CORES
SPREAD = X * Y

PLANES = [[xy * STEP + zc for xy in range(X * Y)] for zc in range(STEP)]
COLUMNS = [[xy * STEP + z * CORES + c for z in range(Z)] for xy in range(X * Y) for c in range(CORES)]


def shifted(value, steps):
    return lax.ppermute(value, "pairs", [(source, (source + steps) % COUNT) for source in range(COUNT)])


def other_core(value):
    return lax.ppermute(value, "pairs", [(source, source ^ 1) for source in range(COUNT)])


def exchange(value, groups):
    return lax.all_to_all(value, "pairs", 0, 0, axis_index_groups=groups, tiled=True)


def embed_kernel(xi_hbm, xt_hbm, wi_hbm, wt_hbm, both_ref, u_ref, x_ref, w_ref, sems):
    rows, width = xi_hbm.shape
    piece = both_ref.shape[1] // 2
    copies = []
    for k, (x_hbm, w_hbm) in enumerate(((xi_hbm, wi_hbm), (xt_hbm, wt_hbm))):
        copies.append(pltpu.make_async_copy(x_hbm, x_ref.at[k], sems.at[k, 0]))
        copies.append(pltpu.make_async_copy(w_hbm, w_ref.at[k], sems.at[k, 1]))
    for copy in copies:
        copy.start()
    for k in range(2):
        copies[2 * k].wait()
        copies[2 * k + 1].wait()
        proj = jnp.dot(x_ref[k], w_ref[k], preferred_element_type=jnp.float32)
        norms = jnp.sqrt(jnp.sum(proj * proj, axis=-1, keepdims=True) + EPS)
        z = (proj / norms).astype(jnp.bfloat16)
        u_ref[k * rows : (k + 1) * rows, :] = proj
        both_ref[:, k * piece : (k + 1) * piece, :] = z.reshape(SPREAD, piece, width)


def embed(image_feats, text_feats, image_head, text_head):
    rows, width = image_feats.shape
    vmem = pl.BlockSpec(memory_space=pltpu.VMEM)
    return pl.pallas_call(
        embed_kernel,
        out_shape=(
            jax.ShapeDtypeStruct((SPREAD, 2 * rows // SPREAD, width), jnp.bfloat16),
            jax.ShapeDtypeStruct((2 * rows, width), jnp.float32),
        ),
        in_specs=[pl.BlockSpec(memory_space=pl.ANY)] * 4,
        out_specs=(vmem,) * 2,
        scratch_shapes=[
            pltpu.VMEM((2, rows, width), jnp.bfloat16),
            pltpu.VMEM((2, width, width), jnp.bfloat16),
            pltpu.SemaphoreType.DMA((2, 2)),
        ],
        compiler_params=pltpu.CompilerParams(vmem_limit_bytes=60 * 1024 * 1024),
        name="embed",
    )(image_feats, text_feats, image_head, text_head)


def turned(value, steps):
    pairs = [(source, source // STEP * STEP + (source + steps) % STEP) for source in range(COUNT)]
    return lax.ppermute(value, "pairs", pairs)


def along(txt, img, low):
    def branch(steps):
        if steps == 0:
            return lambda txt, img: (txt, img)
        return lambda txt, img: (turned(txt, -steps), turned(img, steps))

    return tuple(lax.switch(low, [branch(k) for k in range(STEP)], txt, img))


def line_up_kernel(at_ref, a_ref, b_ref, c_ref, d_ref, out_ref):
    piece = a_ref.shape[1]
    for k, ref in enumerate((a_ref, b_ref, c_ref, d_ref)):
        for p in range(SPREAD):
            out_ref[p, k * piece : (k + 1) * piece, :] = ref[lax.rem(at_ref[k] + p, SPREAD)]


def line_up(at, parts):
    vmem = pl.BlockSpec(memory_space=pltpu.VMEM)
    slots, piece, width = parts[0].shape
    return pl.pallas_call(
        line_up_kernel,
        out_shape=jax.ShapeDtypeStruct((slots, len(parts) * piece, width), parts[0].dtype),
        in_specs=[pl.BlockSpec(memory_space=pltpu.SMEM)] + [vmem] * len(parts),
        out_specs=vmem,
        compiler_params=pltpu.CompilerParams(vmem_limit_bytes=16 * 1024 * 1024),
        name="line_up",
    )(at, *parts)


def fetch(both, offsets):
    piece = both.shape[1] // 2
    place = lax.axis_index("pairs") % STEP
    spread, ahead, behind = lax.optimization_barrier((exchange(both, PLANES), shifted(both, -1), shifted(both, 1)))
    img, txt = spread[:, :piece], spread[:, piece:]

    def turns(low):
        return jnp.minimum(jnp.mod(low, STEP), jnp.mod(-low, STEP))

    swap = turns(offsets[0]) > turns(offsets[1])
    one = jnp.where(swap, offsets[1], offsets[0])
    two = jnp.where(swap, offsets[0], offsets[1])
    one_txt, one_img = along(txt, img, jnp.mod(one, STEP))
    chain = turns(two - one) < turns(two)
    two_txt, two_img = along(
        jnp.where(chain, one_txt, txt),
        jnp.where(chain, one_img, img),
        jnp.mod(jnp.where(chain, two - one, two), STEP),
    )
    at = []
    for offset in (one, two):
        low, high = offset % STEP, offset // STEP
        at += [jnp.mod(high + (place + low) // STEP, SPREAD), jnp.mod(SPREAD - high - (place < low), SPREAD)]
    far = line_up(jnp.stack(at).astype(jnp.int32), (one_txt, one_img, two_txt, two_img))
    return ahead, behind, exchange(far, PLANES)


def dot_t(left, right):
    return lax.dot_general(left, right, (((1,), (1,)), ((), ())), preferred_element_type=jnp.float32)


def piece_of(ref, k, count=2):
    slots, rows, width = ref.shape
    rows = rows // count
    return ref[:, k * rows : (k + 1) * rows, :].reshape(slots * rows, width)


def fold(x):
    return jnp.sum(x.reshape(x.shape[0] // 8, 8, x.shape[1]), axis=0)


def gate(sb_ref, cosine, own):
    logit = sb_ref[0] * cosine + sb_ref[1]
    v = logit if own is None else jnp.where(own, -logit, logit)
    e = jnp.exp(-jnp.abs(v))
    inv = 1.0 / (1.0 + e)
    dlogit = jnp.where(v >= 0, inv, e * inv)
    if own is not None:
        dlogit = jnp.where(own, -dlogit, dlogit)
    return jnp.maximum(v, 0.0) + jnp.log1p(e), dlogit


def tile_pair(sb_ref, zi, zt, txt, img, own=None):
    cosine = dot_t(zi, txt)
    loss, dlogit = gate(sb_ref, cosine, own)
    coef = (sb_ref[0] * dlogit).astype(jnp.bfloat16)
    if own is None:
        coef_back = (sb_ref[0] * gate(sb_ref, dot_t(zt, img), None)[1]).astype(jnp.bfloat16)
    else:
        coef_back = coef.T
    to_img = jnp.dot(coef, txt, preferred_element_type=jnp.float32)
    to_txt = jnp.dot(coef_back, img, preferred_element_type=jnp.float32)
    return to_img, to_txt, fold(loss), fold(dlogit * cosine), fold(dlogit)


def added(left, right):
    return [a + b for a, b in zip(left, right)]


def near_kernel(sb_ref, both_ref, ahead_ref, behind_ref, dz_ref, stats_ref):
    zi, zt = piece_of(both_ref, 0), piece_of(both_ref, 1)
    rows = zi.shape[0]
    own = lax.broadcasted_iota(jnp.int32, (rows, rows), 0) == lax.broadcasted_iota(jnp.int32, (rows, rows), 1)
    sums = tile_pair(sb_ref, zi, zt, zt, zi, own)
    sums = added(sums, tile_pair(sb_ref, zi, zt, piece_of(ahead_ref, 1), piece_of(behind_ref, 0)))
    sums = added(sums, tile_pair(sb_ref, zi, zt, piece_of(behind_ref, 1), piece_of(ahead_ref, 0)))
    for k in range(2):
        dz_ref[k] = sums[k]
    for k in range(3):
        stats_ref[k] = sums[2 + k]


def near(sb, *arrays):
    slots, rows, width = arrays[0].shape
    rows = slots * rows // 2
    vmem = pl.BlockSpec(memory_space=pltpu.VMEM)
    return pl.pallas_call(
        near_kernel,
        out_shape=(
            jax.ShapeDtypeStruct((2, rows, width), jnp.float32),
            jax.ShapeDtypeStruct((3, 8, rows), jnp.float32),
        ),
        in_specs=[pl.BlockSpec(memory_space=pltpu.SMEM)] + [vmem] * len(arrays),
        out_specs=(vmem, vmem),
        compiler_params=pltpu.CompilerParams(vmem_limit_bytes=32 * 1024 * 1024),
        cost_estimate=pl.CostEstimate(flops=30 * rows * rows * width, bytes_accessed=8 * rows * width * 2, transcendentals=0),
        name="near",
    )(sb, *arrays)


def last_kernel(sb_ref, core_ref, both_ref, far_ref, stats_ref, dz_hbm, u_hbm, xi_hbm, xt_hbm,
                dui_ref, dut_ref, kept_ref, given_ref, dz_ref, u_ref, x_ref, sems):
    copies = [
        pltpu.make_async_copy(u_hbm, u_ref, sems.at[0]),
        pltpu.make_async_copy(xi_hbm, x_ref.at[0], sems.at[1]),
        pltpu.make_async_copy(xt_hbm, x_ref.at[1], sems.at[2]),
        pltpu.make_async_copy(dz_hbm, dz_ref, sems.at[3]),
    ]
    for copy in copies:
        copy.start()
    zi, zt = piece_of(both_ref, 0), piece_of(both_ref, 1)
    rows, width = zi.shape
    sums = tile_pair(sb_ref, zi, zt, piece_of(far_ref, 0, 4), piece_of(far_ref, 1, 4))
    sums = added(sums, tile_pair(sb_ref, zi, zt, piece_of(far_ref, 2, 4), piece_of(far_ref, 3, 4)))
    copies[0].wait()
    copies[3].wait()
    for k, du_ref in enumerate((dui_ref, dut_ref)):
        dz = dz_ref[k] + sums[k]
        proj = u_ref[k * rows : (k + 1) * rows, :]
        norms = jnp.sqrt(jnp.sum(proj * proj, axis=-1, keepdims=True) + EPS)
        zh = proj / norms
        inner = jnp.sum(zh * dz, axis=-1, keepdims=True)
        du_ref[...] = ((dz - zh * inner) / norms).astype(jnp.bfloat16)
    copies[1].wait()
    copies[2].wait()

    def head_grad(out_ref, x, du_ref):
        out_ref[0:width, :] = lax.dot_general(
            x, du_ref[...], (((0,), (0,)), ((), ())), preferred_element_type=jnp.float32
        ).astype(out_ref.dtype)

    core = core_ref[0]

    @pl.when(core == 0)
    def _():
        head_grad(given_ref, x_ref[1], dut_ref)
        head_grad(kept_ref, x_ref[0], dui_ref)

    @pl.when(core == 1)
    def _():
        head_grad(given_ref, x_ref[0], dui_ref)
        head_grad(kept_ref, x_ref[1], dut_ref)

    loss, gscale, gbias = (jnp.sum(stats_ref[k] + sums[2 + k]) for k in range(3))
    row = lax.broadcasted_iota(jnp.int32, (16, width), 0)
    at = lax.broadcasted_iota(jnp.int32, (16, width), 1)
    stats = jnp.where(at == 0, loss, jnp.where(at == 1, gscale, gbias))
    stats = jnp.where(at < 3, stats, 0.0)
    kept_ref[width : width + 8, :] = stats[0:8]
    one = stats.astype(jnp.bfloat16).astype(jnp.float32)
    two = (stats - one).astype(jnp.bfloat16).astype(jnp.float32)
    terms = jnp.where(row == 0, one, jnp.where(row == 1, two, jnp.where(row == 2, stats - one - two, 0.0)))
    given_ref[width : width + 16, :] = terms.astype(jnp.bfloat16)


def last(sb, core, both, far, dz, stats, u, image_feats, text_feats):
    rows, width = image_feats.shape
    vmem = pl.BlockSpec(memory_space=pltpu.VMEM)
    return pl.pallas_call(
        last_kernel,
        out_shape=(
            jax.ShapeDtypeStruct((rows, width), jnp.bfloat16),
            jax.ShapeDtypeStruct((rows, width), jnp.bfloat16),
            jax.ShapeDtypeStruct((width + 8, width), jnp.float32),
            jax.ShapeDtypeStruct((width + 16, width), jnp.bfloat16),
        ),
        in_specs=[pl.BlockSpec(memory_space=pltpu.SMEM)] * 2 + [vmem] * 3 + [pl.BlockSpec(memory_space=pl.ANY)] * 4,
        out_specs=(vmem,) * 4,
        scratch_shapes=[
            pltpu.VMEM((2, rows, width), jnp.float32),
            pltpu.VMEM((2 * rows, width), jnp.float32),
            pltpu.VMEM((2, rows, width), jnp.bfloat16),
            pltpu.SemaphoreType.DMA((4,)),
        ],
        compiler_params=pltpu.CompilerParams(vmem_limit_bytes=49 * 1024 * 1024),
        name="last",
    )(sb, core, both, far, stats, dz, u, image_feats, text_feats)


def terms_of(stats):
    one = lax.reduce_precision(stats, 8, 7)
    two = lax.reduce_precision(stats - one, 8, 7)
    return jnp.concatenate([one, two, stats - one - two]).astype(jnp.bfloat16)


def summed_heads(got, kept, total):
    width = kept.shape[1]
    rows = width // (X * Y)
    part = (kept[:width] + got[:width].astype(jnp.float32)).astype(jnp.bfloat16)
    stats = kept[width, 0:3] + jnp.sum(got[width : width + 3, 0:3].astype(jnp.float32), axis=0)
    extra = jnp.zeros((8, width), jnp.bfloat16).at[0, 0:9].set(terms_of(stats))
    plane = jnp.concatenate([part.reshape(X * Y, rows, width), jnp.broadcast_to(extra[None], (X * Y, 8, width))], axis=1)
    plane = exchange(plane, PLANES)
    plane = jnp.sum(plane.astype(jnp.float32), axis=0)
    stats = jnp.sum(plane[rows, 0:9].reshape(3, 3), axis=0)
    few = rows // Z
    extra = jnp.zeros((8 - few, width), jnp.bfloat16).at[0, 0:9].set(terms_of(stats))
    part = plane[:rows].astype(jnp.bfloat16).reshape(Z, few, width)
    column = jnp.concatenate([part, jnp.broadcast_to(extra[None], (Z, 8 - few, width))], axis=1)
    column = jnp.sum(exchange(column, COLUMNS).astype(jnp.float32), axis=0) / total
    stats = jnp.sum(column[few, 0:9].reshape(3, 3), axis=0)
    part = column[:few].astype(jnp.bfloat16)
    part = exchange(jnp.broadcast_to(part[None], (Z, few, width)), COLUMNS).reshape(rows, width)
    part = exchange(jnp.broadcast_to(part[None], (X * Y, rows, width)), PLANES).reshape(width, width)
    return part, stats


def write_kernel(turn, core_ref, part_ref, *refs):
    img_hbm, txt_hbm, wide_ref, sems = refs[-4:]
    rows = part_ref.shape[0] // sems.shape[0]

    def write(out_hbm):
        copies = []
        for k in range(sems.shape[0]):
            at = slice(k * rows, (k + 1) * rows)
            wide_ref[at, :] = part_ref[at, :].astype(jnp.float32)
            copies.append(pltpu.make_async_copy(wide_ref.at[at, :], out_hbm.at[at, :], sems.at[k]))
            copies[-1].start()
        for copy in copies:
            copy.wait()

    @pl.when(core_ref[0] == turn)
    def _():
        write(img_hbm)

    @pl.when(core_ref[0] != turn)
    def _():
        write(txt_hbm)


def write_head(turn, core, part, outs=()):
    width = part.shape[1]
    hbm = pl.BlockSpec(memory_space=pl.ANY)
    return pl.pallas_call(
        functools.partial(write_kernel, turn),
        out_shape=(jax.ShapeDtypeStruct(part.shape, jnp.float32),) * 2,
        in_specs=[pl.BlockSpec(memory_space=pltpu.SMEM), pl.BlockSpec(memory_space=pltpu.VMEM)] + [hbm] * len(outs),
        out_specs=(hbm, hbm),
        scratch_shapes=[pltpu.VMEM(part.shape, jnp.float32), pltpu.SemaphoreType.DMA((8,))],
        input_output_aliases={2 + k: k for k in range(len(outs))},
        compiler_params=pltpu.CompilerParams(vmem_limit_bytes=16 * 1024 * 1024),
        cost_estimate=pl.CostEstimate(flops=width * width, bytes_accessed=6 * width * width, transcendentals=0),
        name="write_head",
    )(core, part, *outs)


def local(image_feats, text_feats, image_head, text_head, logit_scale, logit_bias, round_offsets):
    total = float(COUNT * image_feats.shape[0])
    both, u = embed(image_feats, text_feats, image_head, text_head)
    order = jnp.sort(round_offsets)
    ahead, behind, far = fetch(both, (order[1], order[2]))
    sb = jnp.concatenate([logit_scale, logit_bias])
    core = lax.axis_index("pairs") % CORES
    dz, stats = near(sb, both, ahead, behind)
    du_img, du_txt, kept, given = last(sb, core.reshape(1), both, far, dz, stats, u, image_feats, text_feats)
    g_img = jnp.dot(du_img, image_head.T, preferred_element_type=jnp.float32).astype(jnp.bfloat16)
    g_txt = jnp.dot(du_txt, text_head.T, preferred_element_type=jnp.float32).astype(jnp.bfloat16)
    got, g_img, g_txt = lax.optimization_barrier((other_core(given), g_img, g_txt))
    part, sum_stats = summed_heads(got, kept, total)
    theirs, outs = lax.optimization_barrier((other_core(part), write_head(0, core.reshape(1), part)))
    sum_wi, sum_wt = write_head(1, core.reshape(1), theirs, outs)
    return (g_img, g_txt, sum_wi, sum_wt, sum_stats)


def solution(mesh):
    placed = (P("pairs", None), P("pairs", None), P(), P(), P(), P(), P())
    return jax.shard_map(
        local,
        mesh=mesh,
        in_specs=placed,
        out_specs=(P("pairs", None), P("pairs", None), P(), P(), P()),
        check_vma=False,
    )
```
